256 devices in a mesh: grp: 2 (over core), dp: 64 (over z, x, y_lo), mp: 2 (over y_hi).
Axes of the slice: x: 4, y: 4 (y_hi: 2, y_lo: 2; y = y_hi * 2 + y_lo), z: 8, core: 2. Of those that a mesh axis runs over, the one named last changes fastest.
Arguments:
- image_features: bfloat16 [16384, 1152], P('dp'), may hold values from -8 to 8
- text_features: bfloat16 [16384, 1152], P('dp'), may hold values from -8 to 8
- norm_gain: float32 [2, 1152], P('grp'), may hold values from 0.25 to 1.75
- up_weight: bfloat16 [2, 1152, 4304], P('grp', None, 'mp'), may hold values from -0.1875 to 0.1875
- down_weight: bfloat16 [2, 4304, 1152], P('grp', 'mp'), may hold values from -0.09375 to 0.09375
- text_head: bfloat16 [2, 1152, 1152], P('grp', 'mp'), may hold values from -1 to 2
- sub_index: int32 [2048], replicated, may hold values from 0 to 16383, as said below
Outputs:
- learnability: float32 [16384], P(('dp', 'mp'))
- image_grad: float32 [16384, 1152], P(('dp', 'mp'), 'grp')
The draws below stay inside these ranges and needn't reach their ends.
Inputs may be any that keep to these rules, and one draw needn't show every extreme that they name: `sub_index`: distinct rows in ascending order. Each aligned block of 128 rows holds at most 32 sub-batch rows, and some block holds exactly 32.
All inputs are finite; a program needn't handle non-finite values.
Results may differ from the reference program's by a relative error of at most 0.0067.
Values may be sent and summed in bfloat16 or wider, within the bound.
No kernel may reach another device: no remote copies, remote signals or barrier semaphores. Data moves between devices by JAX's collectives and lax.ppermute only.
A program may use at most 128 MiB of HBM per device.

```python
import math
import jax
import jax.numpy as jnp
from jax import lax

D = 1152
FF = 4304
B = 16384
ROWS = 128
CAP = 32
SUB = 2048


def shared_rows(key, amplitude, low_scale, high_scale):
    key_dir, key_amp, key_jitter, key_scale = jax.random.split(jax.random.fold_in(key, 5), 4)
    directions = jax.random.normal(key_dir, (4, D), jnp.float32)
    weights = amplitude * jax.random.normal(key_amp, (B, 4), jnp.float32)
    common = jnp.zeros((B, D), jnp.float32)
    for number in range(4):
        common = common + weights[:, number:number + 1] * directions[number][None, :]
    jitter = jax.random.normal(key_jitter, (B, D), jnp.float32)
    spread = jnp.exp(jax.random.uniform(key_scale, (B, 1), jnp.float32, math.log(low_scale), math.log(high_scale)))
    return spread * (common + jitter)


def draw_image_features(key, part):
    shared = shared_rows(key, 0.18, 1.0, 1.0)
    return jnp.clip(shared, -8.0, 8.0).astype(jnp.bfloat16)


def draw_text_features(key, part):
    shared = shared_rows(key, 0.18, 1.0, 1.0)
    key = jax.random.fold_in(key, 3)
    caption = 0.7 * jax.random.normal(key, (B, D), jnp.float32)
    return jnp.clip(shared + caption, -8.0, 8.0).astype(jnp.bfloat16)


def draw_text_head(key, part):
    key = jax.random.fold_in(key, 23)
    key_off, key_diag = jax.random.split(key)
    spread = 0.45
    lowest = 0.8
    highest = 1.2
    beside = spread * jnp.clip(jax.random.normal(key_off, (2, D, D), jnp.float32), -4.0, 4.0) * D ** (-0.5)
    middle = jax.random.uniform(key_diag, (2, D, 1), jnp.float32, lowest, highest)
    places = jnp.arange(D, dtype=jnp.int32)
    identity = (places[:, None] == places[None, :]).astype(jnp.float32)
    return (beside + identity[None, :, :] * middle).astype(jnp.bfloat16)


def draw_sub_index(key, part):
    key = jax.random.fold_in(key, 11)
    blocks = B // ROWS
    key_counts, key_ranks = jax.random.split(key)
    pattern = jnp.array([CAP, 3 * CAP // 4, CAP // 4, 0], dtype=jnp.int32)
    counts = jnp.tile(pattern, blocks // 4)[jax.random.permutation(key_counts, blocks)]
    ranks = jax.vmap(lambda k: jax.random.permutation(k, ROWS))(jax.random.split(key_ranks, blocks))
    picked = (ranks < counts[:, None]).reshape(-1)
    return jnp.nonzero(picked, size=SUB)[0].astype(jnp.int32)


def levels(stream_key, extent, pieces, least, largest):
    level = 1.0
    for position, shards_of in pieces:
        heights = jax.random.uniform(jax.random.fold_in(jax.random.fold_in(stream_key, 6), position), (shards_of,), jnp.float32, least / len(pieces), largest / len(pieces))
        level = level * jnp.repeat(jnp.exp(heights), extent[position] // shards_of).reshape((-1,) + (1,) * (len(extent) - 1 - position))
    return level


def centred(own_key, extent, deviation, limit, pieces=(), held_as=jnp.bfloat16):
    factor_of = levels(own_key, extent, pieces, -0.22, 0.18) if pieces else 1.0
    entries = jax.random.normal(own_key, extent, jnp.float32) * deviation * factor_of
    return jnp.minimum(jnp.maximum(entries, -limit), limit).astype(held_as)


def setup_inputs(seed: int = 0) -> dict:
    key_list = jax.random.split(jax.random.key(seed), 8)
    return {
        "image_features": draw_image_features(jax.random.fold_in(key_list[7], 71), 0),
        "text_features": draw_text_features(jax.random.fold_in(key_list[7], 71), 0),
        "norm_gain": jnp.clip(1.0 + 0.15 * jax.random.normal(key_list[2], (2, D), jnp.float32), 0.25, 1.75),
        "up_weight": centred(key_list[3], (2, D, FF), D ** -0.5, 0.1875, ((0, 2), (2, 2))),
        "down_weight": centred(key_list[4], (2, FF, D), FF ** -0.5, 0.09375, ((0, 2), (1, 2))),
        "text_head": draw_text_head(jax.random.fold_in(key_list[7], 71), 0),
        "sub_index": draw_sub_index(jax.random.fold_in(key_list[7], 71), 0),
    }


SCALE = 117.0
BIAS = -12.9
EPS = 1e-06

def embed(image_features, text_features, gain, up, down, head):
    x = image_features.astype(jnp.float32)
    mean = lax.optimization_barrier(jnp.mean(x, axis=1, keepdims=True))
    var = lax.optimization_barrier(jnp.mean((x - mean) * (x - mean), axis=1, keepdims=True))
    normed = ((x - mean) * lax.rsqrt(var + EPS) * gain[None, :]).astype(jnp.bfloat16)
    hidden = jax.nn.gelu(jnp.dot(normed, up, preferred_element_type=jnp.float32), approximate=True).astype(jnp.bfloat16)
    e_img = x + jnp.dot(hidden, down, preferred_element_type=jnp.float32)
    e_txt = jnp.dot(text_features, head, preferred_element_type=jnp.float32)
    n_img = jnp.sqrt(lax.optimization_barrier(jnp.sum(e_img * e_img, axis=1, keepdims=True)) + EPS)
    n_txt = jnp.sqrt(lax.optimization_barrier(jnp.sum(e_txt * e_txt, axis=1, keepdims=True)) + EPS)
    unit = e_img / n_img
    return (unit, n_img, unit.astype(jnp.bfloat16), (e_txt / n_txt).astype(jnp.bfloat16))

def row_losses(z_img, z_txt):
    block = min(512, B)
    count = B // block
    texts_t = z_txt.T
    cols = jnp.arange(B, dtype=jnp.int32)

    def one(index):
        start = (index * block).astype(jnp.int32)
        rows = lax.dynamic_slice_in_dim(z_img, start, block, 0)
        logits = SCALE * jnp.dot(rows, texts_t, preferred_element_type=jnp.float32) + BIAS
        ids = start + jnp.arange(block, dtype=jnp.int32)
        sign = jnp.where(ids[:, None] == cols[None, :], 1.0, -1.0).astype(jnp.float32)
        return lax.optimization_barrier(jnp.sum(jax.nn.softplus(-sign * logits), axis=1))
    return lax.map(one, jnp.arange(count, dtype=jnp.int32)).reshape(B)

def reference(image_features, text_features, norm_gain, up_weight, down_weight, text_head, sub_index):
    unit_0, n_0, z_img_0, z_txt_0 = embed(image_features, text_features, norm_gain[0], up_weight[0], down_weight[0], text_head[0])
    unit_1, n_1, z_img_1, z_txt_1 = embed(image_features, text_features, norm_gain[1], up_weight[1], down_weight[1], text_head[1])
    learnability = row_losses(z_img_1, z_txt_1) - row_losses(z_img_0, z_txt_0)
    img_sub = z_img_1[sub_index]
    txt_sub = z_txt_1[sub_index]
    logits = SCALE * jnp.dot(img_sub, txt_sub.T, preferred_element_type=jnp.float32) + BIAS
    pos = jnp.arange(SUB, dtype=jnp.int32)
    sign = jnp.where(pos[:, None] == pos[None, :], 1.0, -1.0).astype(jnp.float32)
    slope = (-sign * jax.nn.sigmoid(-sign * logits)).astype(jnp.bfloat16)
    g_sub = SCALE * jnp.dot(slope, txt_sub, preferred_element_type=jnp.float32)
    g = jnp.zeros((B, D), jnp.float32).at[sub_index].set(g_sub)
    image_grad = (g - unit_1 * lax.optimization_barrier(jnp.sum(unit_1 * g, axis=1, keepdims=True))) / n_1
    return (learnability, image_grad)
```

```python
import jax
import jax.numpy as jnp
from jax import lax
from jax.experimental import pallas as pl
from jax.experimental.pallas import tpu as pltpu
from jax.sharding import Mesh, PartitionSpec as P

SCALE = 117.0
BIAS = -12.9
EPS = 1e-06
LOG2E = 1.4426950408889634
LN2 = 0.6931471805599453
NZ, NX, NY = 8, 4, 4
ROWS = 128
CAP = 32
AXES = ("grp", "z", "x", "ylo", "yhi")
ZOFF = (0, -1, 1, -2, 2, -3, 3, 4)
POFF = (0, -1, 1, 2)
EXACT = lax.Precision.HIGHEST


def place(g, z, x, y):
    return ((g * NZ + z) * NX + x) * NY + (y % 2) * 2 + y // 2


def permute(v, target, cores=(0, 1)):
    perm = [
        (place(g, z, x, y), place(*target(g, z, x, y)))
        for g in cores
        for z in range(NZ)
        for x in range(NX)
        for y in range(NY)
    ]
    return lax.ppermute(v, AXES, perm)


def over_mp(v):
    return permute(v, lambda g, z, x, y: (g, z, x, (y + 2) % NY))


def over_z(v, shifts, cores=(0, 1)):
    return permute(v, lambda g, z, x, y: (g, (z + shifts[g]) % NZ, x, y), cores)


def over_plane(v, shift, first):
    def target(g, z, x, y):
        if g == first:
            return (g, z, (x + shift) % NX, y)
        return (g, z, x, (y + shift) % NY)

    return permute(v, target)


def swap_cores(v):
    return permute(v, lambda g, z, x, y: (1 - g, z, x, y))


def to_reference(v):
    return permute(v, lambda g, z, x, y: (0, z, x, y), (1,))


def ring8(v):
    back, ahead = [v], [v]
    for _ in range(3):
        back.append(over_z(back[-1], (1, 1)))
        ahead.append(over_z(ahead[-1], (-1, -1)))
    return back, ahead


def shape(dims, dtype=jnp.float32):
    return jax.ShapeDtypeStruct(dims, dtype)


def call(kernel, scalars, arrays, outs, flops, mib=8, transcendentals=0, scratch=()):
    vmem = pl.BlockSpec(memory_space=pltpu.VMEM)
    return pl.pallas_call(
        kernel,
        in_specs=[pl.BlockSpec(memory_space=pltpu.SMEM)] * len(scalars) + [vmem] * len(arrays),
        out_specs=[vmem] * len(outs),
        out_shape=outs,
        scratch_shapes=scratch,
        compiler_params=pltpu.CompilerParams(vmem_limit_bytes=mib * 1024 * 1024),
        cost_estimate=pl.CostEstimate(
            flops=flops, bytes_accessed=1 << 20, transcendentals=transcendentals
        ),
    )(*scalars, *arrays)


def index_kernel(sub_ref, chosen_ref, place_ref):
    sub = sub_ref[...]
    line = lax.broadcasted_iota(jnp.int32, (ROWS, sub.shape[1]), 0)
    in_block = jnp.where((sub >> 7) == line, 1.0, 0.0).astype(jnp.bfloat16)
    at_off = jnp.where((sub & 127) == line, 1.0, 0.0).astype(jnp.bfloat16)
    chosen = lax.dot_general(
        in_block, at_off, (((1,), (1,)), ((), ())), preferred_element_type=jnp.float32
    )
    row = lax.broadcasted_iota(jnp.int32, (ROWS, ROWS), 0)
    col = lax.broadcasted_iota(jnp.int32, (ROWS, ROWS), 1)
    upper = jnp.where(row < col, 1.0, 0.0).astype(jnp.bfloat16)
    rank = jnp.dot(chosen.astype(jnp.bfloat16), upper, preferred_element_type=jnp.float32)
    chosen_ref[...] = chosen
    place_ref[...] = jnp.where(chosen > 0.5, rank, -1.0)


def split_rows(acc_ref, m, own_ref, other_ref):
    rows = own_ref.shape[0]
    own_ref[...] = acc_ref[pl.ds(pl.multiple_of(m * rows, rows), rows), :]
    other = acc_ref[pl.ds(pl.multiple_of((1 - m) * rows, rows), rows), :]
    other_ref[...] = other.astype(jnp.bfloat16)


def text_kernel(pos_ref, text_ref, head_ref, own_ref, other_ref, acc_ref):
    depth = head_ref.shape[0]
    m = pos_ref[0]
    text = text_ref[...]
    part = jnp.where(m == 0, text[:, :depth], text[:, depth:])
    acc_ref[...] = jnp.dot(part, head_ref[...], preferred_element_type=jnp.float32)
    split_rows(acc_ref, m, own_ref, other_ref)


def mlp_kernel(
    pos_ref, gain_ref, x_hbm, up_hbm, down_hbm, own_ref, other_ref,
    x_ref, up_ref, down_ref, normed_ref, hidden_ref, acc_ref, sems,
):
    copies = [
        pltpu.make_async_copy(source, target, sems.at[k])
        for k, (source, target) in enumerate(
            [(x_hbm, x_ref), (up_hbm, up_ref), (down_hbm, down_ref)]
        )
    ]
    for c in copies:
        c.start()
    copies[0].wait()
    x = x_ref[...].astype(jnp.float32)
    mean = jnp.mean(x, axis=1, keepdims=True)
    gap = x - mean
    var = jnp.mean(gap * gap, axis=1, keepdims=True)
    normed_ref[...] = (gap * lax.rsqrt(var + EPS) * gain_ref[...]).astype(jnp.bfloat16)
    copies[1].wait()
    total, block = up_ref.shape[0], 512
    for start in range(0, total, block):
        stop = min(start + block, total)
        acc = lax.dot_general(
            normed_ref[...],
            up_ref[start:stop, :],
            (((1,), (1,)), ((), ())),
            preferred_element_type=jnp.float32,
        )
        hidden_ref[:, start:stop] = jax.nn.gelu(acc, approximate=True).astype(jnp.bfloat16)
    copies[2].wait()
    block = 384
    for start in range(0, acc_ref.shape[1], block):
        acc_ref[:, start : start + block] = jnp.dot(
            hidden_ref[...], down_ref[:, start : start + block], preferred_element_type=jnp.float32
        )
    split_rows(acc_ref, pos_ref[0], own_ref, other_ref)


def image_mlp(pos, gain, x, up, down):
    rows, width = x.shape
    hidden = up.shape[0]
    bf16 = jnp.bfloat16
    vmem, hbm = pl.BlockSpec(memory_space=pltpu.VMEM), pl.BlockSpec(memory_space=pl.ANY)
    return pl.pallas_call(
        mlp_kernel,
        in_specs=[pl.BlockSpec(memory_space=pltpu.SMEM), vmem, hbm, hbm, hbm],
        out_specs=[vmem, vmem],
        out_shape=[shape((rows // 2, width)), shape((rows // 2, width), bf16)],
        scratch_shapes=[
            pltpu.VMEM((rows, width), bf16),
            pltpu.VMEM((hidden, width), bf16),
            pltpu.VMEM((hidden, width), bf16),
            pltpu.VMEM((rows, width), bf16),
            pltpu.VMEM((rows, hidden), bf16),
            pltpu.VMEM((rows, width), jnp.float32),
            pltpu.SemaphoreType.DMA((3,)),
        ],
        compiler_params=pltpu.CompilerParams(vmem_limit_bytes=52 * 1024 * 1024),
        cost_estimate=pl.CostEstimate(
            flops=4 * rows * width * hidden, bytes_accessed=11 << 20, transcendentals=rows * hidden
        ),
    )(pos, gain, x, up, down)


def text_unit_kernel(own_ref, recv_ref, z_ref):
    e = own_ref[...] + recv_ref[...].astype(jnp.float32)
    n = jnp.sqrt(jnp.sum(e * e, axis=1, keepdims=True) + EPS)
    z_ref[...] = (e / n).astype(jnp.bfloat16)


def own_pick(place_row):
    slot = lax.broadcasted_iota(jnp.int32, (CAP, ROWS), 0).astype(jnp.float32)
    return jnp.where(place_row == slot, 1.0, 0.0)


def image_unit_kernel(
    pos_ref, own_ref, recv_ref, x_ref, place_ref, z_ref, unit_ref, n_ref, give_ref
):
    rows = own_ref.shape[0]
    x = x_ref[pl.ds(pl.multiple_of(pos_ref[0] * rows, rows), rows), :].astype(jnp.float32)
    e = x + (own_ref[...] + recv_ref[...].astype(jnp.float32))
    n = jnp.sqrt(jnp.sum(e * e, axis=1, keepdims=True) + EPS)
    unit = e / n
    z_ref[...] = unit.astype(jnp.bfloat16)
    pick = own_pick(place_ref[pl.ds(pos_ref[1] * (NX * NY) + pos_ref[4], 1), :])
    unit = jnp.dot(pick, unit, precision=EXACT, preferred_element_type=jnp.float32)
    n_rows = jnp.broadcast_to(n, (rows, n_ref.shape[1]))
    n_sub = jnp.dot(pick, n_rows, precision=EXACT, preferred_element_type=jnp.float32)
    n_sub = jnp.where(n_sub > 0.0, n_sub, 1.0)
    unit_ref[...] = unit
    n_ref[...] = n_sub
    cut = unit.shape[1] // 2
    give_ref[:, :cut] = unit[:, :cut]
    give_ref[:, cut:] = n_sub


def join_kernel(*refs):
    refs[-1][...] = jnp.concatenate([r[...] for r in refs[:-1]], axis=0)


def fold_terms(e):
    n = e.shape[0]
    while n > 1:
        n //= 2
        a, b = e[:n], e[n:]
        e = a + (b + a * b)
    return e[0]


def tile_loss(text, img, own):
    rows, width = text.shape[0], img.shape[0]
    t = lax.dot_general(text, img, (((1,), (1,)), ((), ())), preferred_element_type=jnp.float32)
    t = t * (SCALE * LOG2E) + (BIAS * LOG2E)
    if own:
        row = lax.broadcasted_iota(jnp.int32, (ROWS, width), 0)
        col = lax.broadcasted_iota(jnp.int32, (ROWS, width), 1)
        t = jnp.concatenate([jnp.where(col == row, -t[:ROWS], t[:ROWS]), t[ROWS:]], axis=0)
    t = t.reshape(rows // 8, 8, width)
    high = jnp.sum(jnp.maximum(t, 0.0), axis=0)
    low = jnp.log1p(fold_terms(jnp.exp2(-jnp.abs(t))))
    return high * LN2 + low


def image_row(z, offset):
    return lax.rem(z + (offset + NZ), NZ)


def pair_kernel(pos_ref, chosen_ref, place_ref, *refs):
    images, texts, (loss_ref, keep_ref, give_ref) = refs[:NZ], refs[NZ:-3], refs[-3:]
    z, x, y, xy = pos_ref[1], pos_ref[2], pos_ref[3], pos_ref[4]
    planes = NX * NY
    block = 256
    pieces = [(ref, s) for ref in texts for s in range(0, ref.shape[0], block)]

    picks = [own_pick(place_ref[pl.ds(image_row(z, o) * planes + xy, 1), :]) for o in ZOFF]
    packed = jnp.concatenate(
        [
            jnp.dot(p.astype(jnp.bfloat16), images[k][...], preferred_element_type=jnp.float32)
            for k, p in enumerate(picks)
        ],
        axis=0,
    ).astype(jnp.bfloat16)

    def text_row(dx, dy):
        tx, ty = lax.rem(x + (dx + NX), NX), lax.rem(y + (dy + NY), NY)
        row = z * planes + tx * NY + lax.rem(ty, 2) * 2 + ty // 2
        return chosen_ref[pl.ds(row, 1), :]

    lines = [text_row(dx, dy) for dx in POFF for dy in POFF]
    total = jnp.zeros(packed.shape, jnp.float32)
    for k, (ref, s) in enumerate(pieces):
        text = ref[s : s + block, :]
        mask = jnp.concatenate(lines[2 * k : 2 * k + 2], axis=1)
        t = lax.dot_general(
            packed, text, (((1,), (1,)), ((), ())), preferred_element_type=jnp.float32
        )
        t = t * SCALE + BIAS
        sign = jnp.ones(t.shape, jnp.float32)
        if k == 0:
            own = jnp.concatenate([1.0 - 2.0 * picks[0], sign[:CAP, ROWS:]], axis=1)
            sign = jnp.concatenate([own, sign[CAP:]], axis=0)
        t = sign * t
        e = jnp.exp(-jnp.abs(t))
        s = jnp.where(t >= 0, 1.0, e) / (1.0 + e)
        slope = (sign * s * mask).astype(jnp.bfloat16)
        total = total + jnp.dot(slope, text, preferred_element_type=jnp.float32)
    total = total.astype(jnp.bfloat16)
    cut = keep_ref.shape[1]
    for k, o in enumerate(ZOFF):
        rows = pl.ds(pl.multiple_of(image_row(z, o) * CAP, CAP), CAP)
        give_ref[rows, :] = total[k * CAP : (k + 1) * CAP, :cut]
        keep_ref[rows, :] = total[k * CAP : (k + 1) * CAP, cut:]

    for number in range(NZ // 2):
        img = jnp.concatenate([images[2 * number][...], images[2 * number + 1][...]], axis=0)
        total = jnp.zeros((8, img.shape[0]), jnp.float32)
        for k, (ref, s) in enumerate(pieces):
            total = total + tile_loss(ref[s : s + block, :], img, number == 0 and k == 0)
        total = jnp.sum(total, axis=0, keepdims=True)
        for k in range(2):
            row = image_row(z, ZOFF[2 * number + k])
            loss_ref[pl.ds(row, 1), :] = total[:, k * ROWS : (k + 1) * ROWS]


def load_kernel(pos_ref, keep_ref, recv_ref, loss_ref, out_ref):
    learner = pos_ref[5] == 1
    loss = loss_ref[...]
    parts = []
    for _ in range(3):
        part = loss.astype(jnp.bfloat16)
        loss = loss - part.astype(jnp.float32)
        parts.append(part.astype(jnp.float32))
    side = ROWS // 2
    for z in range(NZ):
        rows = slice(z * CAP, (z + 1) * CAP)
        halves = [p[z : z + 1, k * side : (k + 1) * side] for p in parts for k in range(2)]
        beside = jnp.concatenate(halves + [jnp.zeros((CAP - 6, side), jnp.float32)], axis=0)
        grad = jnp.where(learner, keep_ref[rows, :], recv_ref[rows, :])
        out_ref[rows, :] = jnp.concatenate([grad, beside.astype(jnp.bfloat16)], axis=1)


def finish_kernel(pos_ref, load_ref, unit_ref, given_ref, n_ref, g_ref, msg_ref):
    learner = pos_ref[5] == 1
    cut = g_ref.shape[1]
    total = load_ref[:CAP, :].astype(jnp.float32)
    for z in range(1, NZ):
        total = total + load_ref[z * CAP : (z + 1) * CAP, :].astype(jnp.float32)
    g = SCALE * total[:, :cut]
    unit = jnp.where(learner, unit_ref[:, cut:], given_ref[:, :cut])
    n = jnp.where(learner, n_ref[...], given_ref[:, cut:])
    g_ref[...] = g
    dots = jnp.sum(unit * g, axis=1, keepdims=True)
    beside = total[:, cut:]
    loss = jnp.concatenate(
        [beside[k : k + 1] + beside[k + 2 : k + 3] + beside[k + 4 : k + 5] for k in range(2)], axis=1
    )
    msg_ref[:CAP, :] = jnp.broadcast_to(dots, (CAP, ROWS))
    msg_ref[CAP:, :] = jnp.broadcast_to(loss, (8, ROWS))


def spread_kernel(
    pos_ref, g_ref, unit_ref, given_ref, n_ref, own_ref, other_ref, place_ref, learn_ref, out_ref
):
    learner = pos_ref[5] == 1
    cut = g_ref.shape[1]
    unit = jnp.where(learner, unit_ref[:, cut:], given_ref[:, :cut])
    n = jnp.where(learner, n_ref[...], given_ref[:, cut:])[:, :1]
    dots = (own_ref[:CAP, :] + other_ref[:CAP, :])[:, :1]
    grad = (g_ref[...] - unit * dots) / n
    pick = own_pick(place_ref[pl.ds(pos_ref[1] * (NX * NY) + pos_ref[4], 1), :])
    out_ref[...] = lax.dot_general(
        pick, grad, (((0,), (0,)), ((), ())), precision=EXACT, preferred_element_type=jnp.float32
    )
    own, other = own_ref[CAP : CAP + 1, :], other_ref[CAP : CAP + 1, :]
    learn_ref[...] = jnp.where(learner, own - other, other - own)


def shards(image_features, text_features, norm_gain, up_weight, down_weight, text_head, sub_index):
    g_idx = lax.axis_index("grp")
    z_idx = lax.axis_index("z")
    x_idx = lax.axis_index("x")
    m_idx = lax.axis_index("yhi")
    l_idx = lax.axis_index("ylo")
    width = image_features.shape[1]
    rows = image_features.shape[0] // 2
    blocks = NZ * NX * NY
    cut = width // 2
    bf16 = jnp.bfloat16
    pos = [m_idx, z_idx, x_idx, m_idx * 2 + l_idx, (x_idx * 2 + l_idx) * 2 + m_idx, g_idx]
    pos = jnp.stack([p.astype(jnp.int32) for p in pos])
    cells = rows * width

    own_img, other_img = image_mlp(pos, norm_gain, image_features, up_weight[0].T, down_weight[0])
    recv_img = over_mp(other_img)
    features, own_img = lax.optimization_barrier((text_features, own_img))
    own_text, other_text = call(
        text_kernel,
        [pos],
        [features, text_head[0]],
        [shape((rows, width)), shape((rows, width), bf16)],
        2 * cells * width,
        scratch=[pltpu.VMEM((2 * rows, width), jnp.float32)],
    )
    recv_text = over_mp(other_text)
    chosen, place_of = call(
        index_kernel, [], [sub_index.reshape(1, -1)], [shape((blocks, rows))] * 2, 100 << 20
    )
    z_img, unit_sub, n_sub, give = call(
        image_unit_kernel,
        [pos],
        [own_img, recv_img, image_features, place_of],
        [shape((rows, width), bf16), shape((CAP, width)), shape((CAP, rows)), shape((CAP, cut + rows))],
        400 * cells,
    )
    own_text, z_img = lax.optimization_barrier((own_text, z_img))
    (z_txt,) = call(
        text_unit_kernel, [], [own_text, recv_text], [shape((rows, width), bf16)], 20 * cells
    )
    line = [z_txt] + [over_plane(z_txt, shift, 0) for shift in (1, -1, 2)]
    (joined,) = call(join_kernel, [], line, [shape((4 * rows, width), bf16)], cells)
    back, ahead = over_plane(joined, 1, 1), over_plane(joined, -1, 1)
    far_top = over_plane(back[: 2 * rows], 1, 1)
    far_low = over_plane(ahead[2 * rows :], -1, 1)
    texts = [joined, back, ahead, far_top, far_low]

    from_back, from_ahead = ring8(z_img)
    last = jnp.where(g_idx == 0, from_back[3], from_ahead[3])
    images = [z_img, from_back[1], from_ahead[1], from_back[2], from_ahead[2]]
    images += [from_back[3], from_ahead[3], over_z(last, (1, -1))]

    given = to_reference(give)

    n_text, n_img = NX * NY * rows, NZ * rows
    loss_part, g_keep, g_give = call(
        pair_kernel,
        [pos],
        [chosen, place_of] + images + texts,
        [shape((NZ, rows))] + [shape((NZ * CAP, cut), bf16)] * 2,
        (2 * n_img + 4 * NZ * CAP) * width * n_text,
        mib=16,
        transcendentals=(n_img + NZ * CAP) * n_text,
    )
    (load,) = call(
        load_kernel,
        [pos],
        [g_keep, to_reference(g_give), loss_part],
        [shape((NZ * CAP, cut + rows // 2), bf16)],
        cells,
    )
    load = lax.all_to_all(load, "z", 0, 0, tiled=True)
    g_sum, msg = call(
        finish_kernel,
        [pos],
        [load, unit_sub, given, n_sub],
        [shape((CAP, cut)), shape((CAP + 8, rows))],
        10 * cells,
    )
    learn, image_grad = call(
        spread_kernel,
        [pos],
        [g_sum, unit_sub, given, n_sub, msg, swap_cores(msg), place_of],
        [shape((1, rows)), shape((rows, cut))],
        200 * cells,
    )
    return (learn.reshape(rows), image_grad)


def solution(mesh):
    fine = Mesh(mesh.devices.reshape(2, NZ, NX, 2, 2), AXES)
    dp = ("z", "x", "ylo")
    in_specs = (
        P(dp, None),
        P(dp, None),
        P("grp", None),
        P("grp", None, "yhi"),
        P("grp", "yhi", None),
        P("grp", "yhi", None),
        P(),
    )
    out_specs = (P(dp + ("yhi",)), P(dp + ("yhi",), "grp"))
    return jax.shard_map(shards, mesh=fine, in_specs=in_specs, out_specs=out_specs, check_vma=False)
```

```python
import jax
import jax.numpy as jnp
from jax import lax
from jax.experimental import pallas as pl
from jax.experimental.pallas import tpu as pltpu
from jax.sharding import Mesh, PartitionSpec as P

SCALE = 117.0
BIAS = -12.9
EPS = 1e-06
LOG2E = 1.4426950408889634
LN2 = 0.6931471805599453
NZ, NX, NY = 8, 4, 4
ROWS = 128
CAP = 32
AXES = ("grp", "z", "x", "ylo", "yhi")
ZOFF = (0, -1, 1, -2, 2, -3, 3, 4)
POFF = (0, -1, 1, 2)
EXACT = lax.Precision.HIGHEST


def place(g, z, x, y):
    return ((g * NZ + z) * NX + x) * NY + (y % 2) * 2 + y // 2


def permute(v, target, cores=(0, 1)):
    perm = [
        (place(g, z, x, y), place(*target(g, z, x, y)))
        for g in cores
        for z in range(NZ)
        for x in range(NX)
        for y in range(NY)
    ]
    return lax.ppermute(v, AXES, perm)


def over_mp(v):
    return permute(v, lambda g, z, x, y: (g, z, x, (y + 2) % NY))


def over_z(v, shifts, cores=(0, 1)):
    return permute(v, lambda g, z, x, y: (g, (z + shifts[g]) % NZ, x, y), cores)


def over_plane(v, shift, first):
    def target(g, z, x, y):
        if g == first:
            return (g, z, (x + shift) % NX, y)
        return (g, z, x, (y + shift) % NY)

    return permute(v, target)


def swap_cores(v):
    return permute(v, lambda g, z, x, y: (1 - g, z, x, y))


def shape(dims, dtype=jnp.float32):
    return jax.ShapeDtypeStruct(dims, dtype)


def call(kernel, scalars, arrays, outs, flops, mib=8, transcendentals=0, scratch=()):
    vmem = pl.BlockSpec(memory_space=pltpu.VMEM)
    return pl.pallas_call(
        kernel,
        in_specs=[pl.BlockSpec(memory_space=pltpu.SMEM)] * len(scalars) + [vmem] * len(arrays),
        out_specs=[vmem] * len(outs),
        out_shape=outs,
        scratch_shapes=scratch,
        compiler_params=pltpu.CompilerParams(vmem_limit_bytes=mib * 1024 * 1024),
        cost_estimate=pl.CostEstimate(
            flops=flops, bytes_accessed=1 << 20, transcendentals=transcendentals
        ),
    )(*scalars, *arrays)


def index_kernel(sub_ref, chosen_ref, place_ref):
    sub = sub_ref[...]
    line = lax.broadcasted_iota(jnp.int32, (ROWS, sub.shape[1]), 0)
    in_block = jnp.where((sub >> 7) == line, 1.0, 0.0).astype(jnp.bfloat16)
    at_off = jnp.where((sub & 127) == line, 1.0, 0.0).astype(jnp.bfloat16)
    chosen = lax.dot_general(
        in_block, at_off, (((1,), (1,)), ((), ())), preferred_element_type=jnp.float32
    )
    row = lax.broadcasted_iota(jnp.int32, (ROWS, ROWS), 0)
    col = lax.broadcasted_iota(jnp.int32, (ROWS, ROWS), 1)
    upper = jnp.where(row < col, 1.0, 0.0).astype(jnp.bfloat16)
    rank = jnp.dot(chosen.astype(jnp.bfloat16), upper, preferred_element_type=jnp.float32)
    chosen_ref[...] = chosen
    place_ref[...] = jnp.where(chosen > 0.5, rank, -1.0)


def split_rows(acc_ref, m, own_ref, other_ref):
    rows = own_ref.shape[0]
    own_ref[...] = acc_ref[pl.ds(pl.multiple_of(m * rows, rows), rows), :]
    other = acc_ref[pl.ds(pl.multiple_of((1 - m) * rows, rows), rows), :]
    other_ref[...] = other.astype(jnp.bfloat16)


def text_kernel(
    pos_ref, text_hbm, head_hbm, own_ref, other_ref, text_ref, head_ref, acc_ref, sems
):
    copies = [
        pltpu.make_async_copy(text_hbm, text_ref, sems.at[0]),
        pltpu.make_async_copy(head_hbm, head_ref, sems.at[1]),
    ]
    for c in copies:
        c.start()
    for c in copies:
        c.wait()
    depth = head_ref.shape[0]
    m = pos_ref[0]
    text = text_ref[...]
    part = jnp.where(m == 0, text[:, :depth], text[:, depth:])
    acc_ref[...] = jnp.dot(part, head_ref[...], preferred_element_type=jnp.float32)
    split_rows(acc_ref, m, own_ref, other_ref)


def mlp_kernel(
    pos_ref, gain_hbm, x_hbm, up_hbm, down_hbm, own_ref, other_ref,
    gain_ref, x_ref, up_ref, down_ref, normed_ref, hidden_ref, acc_ref, sems,
):
    copies = [
        pltpu.make_async_copy(source, target, sems.at[k])
        for k, (source, target) in enumerate(
            [(x_hbm, x_ref), (up_hbm, up_ref), (down_hbm, down_ref), (gain_hbm, gain_ref)]
        )
    ]
    for c in copies:
        c.start()
    copies[0].wait()
    x = x_ref[...].astype(jnp.float32)
    mean = jnp.mean(x, axis=1, keepdims=True)
    gap = x - mean
    var = jnp.mean(gap * gap, axis=1, keepdims=True)
    copies[3].wait()
    normed_ref[...] = (gap * lax.rsqrt(var + EPS) * gain_ref[...]).astype(jnp.bfloat16)
    copies[1].wait()
    total, block = up_ref.shape[0], 512
    for start in range(0, total, block):
        stop = min(start + block, total)
        acc = lax.dot_general(
            normed_ref[...],
            up_ref[start:stop, :],
            (((1,), (1,)), ((), ())),
            preferred_element_type=jnp.float32,
        )
        hidden_ref[:, start:stop] = jax.nn.gelu(acc, approximate=True).astype(jnp.bfloat16)
    copies[2].wait()
    block = 384
    for start in range(0, acc_ref.shape[1], block):
        acc_ref[:, start : start + block] = jnp.dot(
            hidden_ref[...], down_ref[:, start : start + block], preferred_element_type=jnp.float32
        )
    split_rows(acc_ref, pos_ref[0], own_ref, other_ref)
    rows = own_ref.shape[0]
    x = x_ref[pl.ds(pl.multiple_of(pos_ref[0] * rows, rows), rows), :]
    own_ref[...] = own_ref[...] + x.astype(jnp.float32)


def from_hbm(kernel, pos, arrays, rows, width, scratch, flops):
    vmem, hbm = pl.BlockSpec(memory_space=pltpu.VMEM), pl.BlockSpec(memory_space=pl.ANY)
    return pl.pallas_call(
        kernel,
        in_specs=[pl.BlockSpec(memory_space=pltpu.SMEM)] + [hbm] * len(arrays),
        out_specs=[vmem, vmem],
        out_shape=[shape((rows, width)), shape((rows, width), jnp.bfloat16)],
        scratch_shapes=[pltpu.VMEM(a.shape, a.dtype) for a in arrays]
        + scratch
        + [pltpu.VMEM((2 * rows, width), jnp.float32), pltpu.SemaphoreType.DMA((len(arrays),))],
        compiler_params=pltpu.CompilerParams(vmem_limit_bytes=52 * 1024 * 1024),
        cost_estimate=pl.CostEstimate(flops=flops, bytes_accessed=11 << 20, transcendentals=0),
    )(pos, *arrays)


def text_unit_kernel(own_ref, recv_ref, z_ref):
    e = own_ref[...] + recv_ref[...].astype(jnp.float32)
    n = jnp.sqrt(jnp.sum(e * e, axis=1, keepdims=True) + EPS)
    z_ref[...] = (e / n).astype(jnp.bfloat16)


def own_pick(place_row):
    slot = lax.broadcasted_iota(jnp.int32, (CAP, ROWS), 0).astype(jnp.float32)
    return jnp.where(place_row == slot, 1.0, 0.0)


def image_unit_kernel(own_ref, recv_ref, z_ref, unit_ref, n_ref):
    e = own_ref[...] + recv_ref[...].astype(jnp.float32)
    n = jnp.sqrt(jnp.sum(e * e, axis=1, keepdims=True) + EPS)
    unit = e / n
    z_ref[...] = unit.astype(jnp.bfloat16)
    unit_ref[...] = unit
    n_ref[...] = jnp.broadcast_to(n, n_ref.shape)


def sub_unit_kernel(pos_ref, unit_ref, n_ref, place_ref, unit_sub_ref, n_sub_ref):
    pick = own_pick(place_ref[pl.ds(pos_ref[1] * (NX * NY) + pos_ref[4], 1), :])
    unit_sub_ref[...] = jnp.dot(
        pick, unit_ref[...], precision=EXACT, preferred_element_type=jnp.float32
    )
    n_sub = jnp.dot(pick, n_ref[...], precision=EXACT, preferred_element_type=jnp.float32)
    n_sub_ref[...] = jnp.where(n_sub > 0.0, n_sub, 1.0)


def join_kernel(*refs):
    refs[-1][...] = jnp.concatenate([r[...] for r in refs[:-1]], axis=0)


def fold_terms(e):
    n = e.shape[0]
    while n > 1:
        n //= 2
        a, b = e[:n], e[n:]
        e = a + (b + a * b)
    return e[0]


def tile_loss(text, img, own):
    rows, width = text.shape[0], img.shape[0]
    t = lax.dot_general(text, img, (((1,), (1,)), ((), ())), preferred_element_type=jnp.float32)
    t = t * (SCALE * LOG2E) + (BIAS * LOG2E)
    if own:
        row = lax.broadcasted_iota(jnp.int32, (ROWS, width), 0)
        col = lax.broadcasted_iota(jnp.int32, (ROWS, width), 1)
        t = jnp.concatenate([jnp.where(col == row, -t[:ROWS], t[:ROWS]), t[ROWS:]], axis=0)
    t = t.reshape(rows // 8, 8, width)
    high = jnp.sum(jnp.maximum(t, 0.0), axis=0)
    low = jnp.log1p(fold_terms(jnp.exp2(-jnp.abs(t))))
    return high * LN2 + low


def image_row(z, offset):
    return lax.rem(z + (offset + NZ), NZ)


def pair_kernel(pos_ref, chosen_ref, place_ref, *refs):
    images, texts, load_ref = refs[:NZ], refs[NZ:-1], refs[-1]
    z, x, y, xy = pos_ref[1], pos_ref[2], pos_ref[3], pos_ref[4]
    planes = NX * NY
    block = 256
    pieces = [(ref, s) for ref in texts for s in range(0, ref.shape[0], block)]

    picks = [own_pick(place_ref[pl.ds(image_row(z, o) * planes + xy, 1), :]) for o in ZOFF]
    packed = jnp.concatenate(
        [
            jnp.dot(p.astype(jnp.bfloat16), images[k][...], preferred_element_type=jnp.float32)
            for k, p in enumerate(picks)
        ],
        axis=0,
    ).astype(jnp.bfloat16)

    def text_row(dx, dy):
        tx, ty = lax.rem(x + (dx + NX), NX), lax.rem(y + (dy + NY), NY)
        row = z * planes + tx * NY + lax.rem(ty, 2) * 2 + ty // 2
        return chosen_ref[pl.ds(row, 1), :]

    lines = [text_row(dx, dy) for dx in POFF for dy in POFF]
    total = jnp.zeros(packed.shape, jnp.float32)
    for k, (ref, s) in enumerate(pieces):
        text = ref[s : s + block, :]
        mask = jnp.concatenate(lines[2 * k : 2 * k + 2], axis=1)
        t = lax.dot_general(
            packed, text, (((1,), (1,)), ((), ())), preferred_element_type=jnp.float32
        )
        t = t * SCALE + BIAS
        sign = jnp.ones(t.shape, jnp.float32)
        if k == 0:
            own = jnp.concatenate([1.0 - 2.0 * picks[0], sign[:CAP, ROWS:]], axis=1)
            sign = jnp.concatenate([own, sign[CAP:]], axis=0)
        t = sign * t
        e = jnp.exp(-jnp.abs(t))
        s = jnp.where(t >= 0, 1.0, e) / (1.0 + e)
        slope = (sign * s * mask).astype(jnp.bfloat16)
        total = total + jnp.dot(slope, text, preferred_element_type=jnp.float32)
    total = total.astype(jnp.bfloat16)
    width = total.shape[1]
    for k, o in enumerate(ZOFF):
        rows = pl.ds(pl.multiple_of(image_row(z, o) * CAP, CAP), CAP)
        load_ref[rows, :width] = total[k * CAP : (k + 1) * CAP, :]

    for number in range(NZ // 2):
        img = jnp.concatenate([images[2 * number][...], images[2 * number + 1][...]], axis=0)
        total = jnp.zeros((8, img.shape[0]), jnp.float32)
        for k, (ref, s) in enumerate(pieces):
            total = total + tile_loss(ref[s : s + block, :], img, number == 0 and k == 0)
        total = jnp.sum(total, axis=0, keepdims=True)
        for k in range(2):
            loss = total[:, k * ROWS : (k + 1) * ROWS]
            parts = []
            for _ in range(3):
                part = loss.astype(jnp.bfloat16).astype(jnp.float32)
                loss = loss - part
                parts.append(part)
            parts.append(jnp.zeros((CAP - 3, ROWS), jnp.float32))
            beside = jnp.concatenate(parts, axis=0).astype(jnp.bfloat16)
            row = image_row(z, ZOFF[2 * number + k])
            load_ref[pl.ds(pl.multiple_of(row * CAP, CAP), CAP), width:] = beside


def finish_kernel(load_ref, unit_ref, n_ref, keep_ref, msg_ref):
    width = unit_ref.shape[1]
    cut = width // 2
    total = load_ref[:CAP, :].astype(jnp.float32)
    for z in range(1, NZ):
        total = total + load_ref[z * CAP : (z + 1) * CAP, :].astype(jnp.float32)
    g = SCALE * total[:, :width]
    unit = unit_ref[...]
    grad = (g - unit * jnp.sum(unit * g, axis=1, keepdims=True)) / n_ref[:, :1]
    loss = total[0:1, width:] + total[1:2, width:] + total[2:3, width:]
    line = jnp.concatenate([loss, jnp.zeros((1, cut - ROWS), jnp.float32)], axis=1)
    keep_ref[:CAP, :] = grad[:, cut:]
    keep_ref[CAP:, :] = jnp.broadcast_to(line, (8, cut))
    msg_ref[:CAP, :] = grad[:, :cut]
    msg_ref[CAP:, :] = jnp.broadcast_to(line, (8, cut))


def spread_kernel(pos_ref, keep_ref, recv_ref, place_ref, learn_ref, out_hbm, out_ref, sem):
    learner = pos_ref[5] == 1
    half = jnp.where(learner, keep_ref[:CAP, :], recv_ref[:CAP, :])
    pick = own_pick(place_ref[pl.ds(pos_ref[1] * (NX * NY) + pos_ref[4], 1), :])
    out_ref[...] = lax.dot_general(
        pick, half, (((0,), (0,)), ((), ())), precision=EXACT, preferred_element_type=jnp.float32
    )
    copy = pltpu.make_async_copy(out_ref, out_hbm, sem)
    copy.start()
    own, other = keep_ref[CAP : CAP + 1, :ROWS], recv_ref[CAP : CAP + 1, :ROWS]
    learn_ref[...] = jnp.where(learner, own - other, other - own)
    copy.wait()


def spread(pos, keep, recv, place_of):
    vmem, hbm = pl.BlockSpec(memory_space=pltpu.VMEM), pl.BlockSpec(memory_space=pl.ANY)
    cut = keep.shape[1]
    return pl.pallas_call(
        spread_kernel,
        in_specs=[pl.BlockSpec(memory_space=pltpu.SMEM)] + [vmem] * 3,
        out_specs=[vmem, hbm],
        out_shape=[shape((1, ROWS)), shape((ROWS, cut))],
        scratch_shapes=[pltpu.VMEM((ROWS, cut), jnp.float32), pltpu.SemaphoreType.DMA(())],
        compiler_params=pltpu.CompilerParams(vmem_limit_bytes=56 * 1024 * 1024),
        cost_estimate=pl.CostEstimate(flops=1 << 24, bytes_accessed=1 << 20, transcendentals=0),
    )(pos, keep, recv, place_of)


def shards(image_features, text_features, norm_gain, up_weight, down_weight, text_head, sub_index):
    g_idx = lax.axis_index("grp")
    z_idx = lax.axis_index("z")
    x_idx = lax.axis_index("x")
    m_idx = lax.axis_index("yhi")
    l_idx = lax.axis_index("ylo")
    width = image_features.shape[1]
    rows = image_features.shape[0] // 2
    blocks = NZ * NX * NY
    cut = width // 2
    bf16 = jnp.bfloat16
    pos = [m_idx, z_idx, x_idx, m_idx * 2 + l_idx, (x_idx * 2 + l_idx) * 2 + m_idx, g_idx]
    pos = jnp.stack([p.astype(jnp.int32) for p in pos])
    cells = rows * width

    own_text, other_text = from_hbm(
        text_kernel, pos, [text_features, text_head[0]], rows, width, [], 2 * cells * width
    )
    recv_text = over_mp(other_text)
    features, own_text = lax.optimization_barrier((image_features, own_text))
    hidden = up_weight.shape[2]
    own_img, other_img = from_hbm(
        mlp_kernel,
        pos,
        [norm_gain, features, up_weight[0].T, down_weight[0]],
        rows,
        width,
        [pltpu.VMEM((2 * rows, width), bf16), pltpu.VMEM((2 * rows, hidden), bf16)],
        8 * cells * hidden,
    )
    recv_img = over_mp(other_img)
    chosen, place_of = call(
        index_kernel, [], [sub_index.reshape(1, -1)], [shape((blocks, rows))] * 2, 100 << 20
    )
    z_img, unit, n_img = call(
        image_unit_kernel,
        [],
        [own_img, recv_img],
        [shape((rows, width), bf16), shape((rows, width)), shape((rows, rows))],
        20 * cells,
    )
    own_text, z_img = lax.optimization_barrier((own_text, z_img))
    (z_txt,) = call(
        text_unit_kernel, [], [own_text, recv_text], [shape((rows, width), bf16)], 20 * cells
    )
    line = [z_txt] + [over_plane(z_txt, shift, 0) for shift in (1, -1, 2)]
    back, ahead = [z_img], [z_img]

    def z_step():
        back.append(over_z(back[-1], (1, 1)))
        ahead.append(over_z(ahead[-1], (-1, -1)))

    z_step()
    line[0], back[1], ahead[1] = lax.optimization_barrier((line[0], back[1], ahead[1]))
    (joined,) = call(join_kernel, [], line, [shape((4 * rows, width), bf16)], cells)
    z_step()
    text_back, text_ahead = over_plane(joined, 1, 1), over_plane(joined, -1, 1)
    z_step()
    text_back, text_ahead, back[3], ahead[3] = lax.optimization_barrier(
        (text_back, text_ahead, back[3], ahead[3])
    )
    last = over_z(jnp.where(g_idx == 0, back[3], ahead[3]), (1, -1))
    far_top = over_plane(text_back[: 2 * rows], 1, 1)
    far_low = over_plane(text_ahead[2 * rows :], -1, 1)
    texts = [joined, text_back, text_ahead, far_top, far_low]
    images = [z_img, back[1], ahead[1], back[2], ahead[2], back[3], ahead[3], last]

    n_pairs, n_text = (NZ * rows, NX * NY * rows)
    (load,) = call(
        pair_kernel,
        [pos],
        [chosen, place_of] + images + texts,
        [shape((NZ * CAP, width + rows), bf16)],
        (2 * n_pairs + 4 * NZ * CAP) * width * n_text,
        mib=16,
        transcendentals=(n_pairs + NZ * CAP) * n_text,
    )
    load = lax.all_to_all(load, "z", 0, 0, tiled=True)
    unit_sub, n_sub = call(
        sub_unit_kernel,
        [pos],
        [unit, n_img, place_of],
        [shape((CAP, width)), shape((CAP, rows))],
        400 * cells,
    )
    keep, msg = call(
        finish_kernel, [], [load, unit_sub, n_sub], [shape((CAP + 8, cut))] * 2, 10 * cells
    )
    learn, image_grad = spread(pos, keep, swap_cores(msg), place_of)
    return (learn.reshape(rows), image_grad)


def solution(mesh):
    fine = Mesh(mesh.devices.reshape(2, NZ, NX, 2, 2), AXES)
    dp = ("z", "x", "ylo")
    in_specs = (
        P(dp, None),
        P(dp, None),
        P("grp", None),
        P("grp", None, "yhi"),
        P("grp", "yhi", None),
        P("grp", "yhi", None),
        P(),
    )
    out_specs = (P(dp + ("yhi",)), P(dp + ("yhi",), "grp"))
    return jax.shard_map(shards, mesh=fine, in_specs=in_specs, out_specs=out_specs, check_vma=False)
```

```python
import jax
import jax.numpy as jnp
from jax import lax
from jax.experimental import pallas as pl
from jax.experimental.pallas import tpu as pltpu
from jax.sharding import Mesh, PartitionSpec as P

SCALE = 117.0
BIAS = -12.9
EPS = 1e-06
LOG2E = 1.4426950408889634
LN2 = 0.6931471805599453
NZ, NX, NY = 8, 4, 4
ROWS = 128
BLOCK = 256
CAP = 32
AXES = ("grp", "z", "x", "ylo", "yhi")
ZOFF = (0, -1, 1, -2, 2, -3, 3, 4)
POFF = (0, -1, 1, 2)
EXACT = lax.Precision.HIGHEST


def place(g, z, x, y):
    return ((g * NZ + z) * NX + x) * NY + (y % 2) * 2 + y // 2


def permute(v, target, cores=(0, 1)):
    perm = [
        (place(g, z, x, y), place(*target(g, z, x, y)))
        for g in cores
        for z in range(NZ)
        for x in range(NX)
        for y in range(NY)
    ]
    return lax.ppermute(v, AXES, perm)


def over_mp(v):
    return permute(v, lambda g, z, x, y: (g, z, x, (y + 2) % NY))


def over_z(v, shifts, cores=(0, 1)):
    return permute(v, lambda g, z, x, y: (g, (z + shifts[g]) % NZ, x, y), cores)


def over_plane(v, shift, first):
    def target(g, z, x, y):
        if g == first:
            return (g, z, (x + shift) % NX, y)
        return (g, z, x, (y + shift) % NY)

    return permute(v, target)


def swap_cores(v):
    return permute(v, lambda g, z, x, y: (1 - g, z, x, y))


def shape(dims, dtype=jnp.float32):
    return jax.ShapeDtypeStruct(dims, dtype)


def call(kernel, scalars, arrays, outs, flops, mib=8, transcendentals=0, scratch=()):
    vmem = pl.BlockSpec(memory_space=pltpu.VMEM)
    return pl.pallas_call(
        kernel,
        in_specs=[pl.BlockSpec(memory_space=pltpu.SMEM)] * len(scalars) + [vmem] * len(arrays),
        out_specs=[vmem] * len(outs),
        out_shape=outs,
        scratch_shapes=scratch,
        compiler_params=pltpu.CompilerParams(vmem_limit_bytes=mib * 1024 * 1024),
        cost_estimate=pl.CostEstimate(
            flops=flops, bytes_accessed=1 << 20, transcendentals=transcendentals
        ),
    )(*scalars, *arrays)


def index_kernel(sub_ref, chosen_ref, place_ref):
    sub = sub_ref[...]
    line = lax.broadcasted_iota(jnp.int32, (ROWS, sub.shape[1]), 0)
    in_block = jnp.where((sub >> 7) == line, 1.0, 0.0).astype(jnp.bfloat16)
    at_off = jnp.where((sub & 127) == line, 1.0, 0.0).astype(jnp.bfloat16)
    chosen = lax.dot_general(
        in_block, at_off, (((1,), (1,)), ((), ())), preferred_element_type=jnp.float32
    )
    row = lax.broadcasted_iota(jnp.int32, (ROWS, ROWS), 0)
    col = lax.broadcasted_iota(jnp.int32, (ROWS, ROWS), 1)
    upper = jnp.where(row < col, 1.0, 0.0).astype(jnp.bfloat16)
    rank = jnp.dot(chosen.astype(jnp.bfloat16), upper, preferred_element_type=jnp.float32)
    chosen_ref[...] = chosen
    place_ref[...] = jnp.where(chosen > 0.5, rank, -1.0)


def split_rows(acc_ref, m, own_ref, other_ref):
    rows = own_ref.shape[0]
    own_ref[...] = acc_ref[pl.ds(pl.multiple_of(m * rows, rows), rows), :]
    other = acc_ref[pl.ds(pl.multiple_of((1 - m) * rows, rows), rows), :]
    other_ref[...] = other.astype(jnp.bfloat16)


def head_kernel(
    pos_ref, x_hbm, gain_hbm, text_hbm, head_hbm, up_hbm, down_hbm,
    own_ref, other_ref, own_text_ref, other_text_ref,
    x_ref, gain_ref, text_ref, head_ref, up_ref, down_ref,
    normed_ref, hidden_ref, acc_ref, sems,
):
    sources = [x_hbm, gain_hbm, text_hbm, head_hbm, up_hbm, down_hbm]
    targets = [x_ref, gain_ref, text_ref, head_ref, up_ref, down_ref]
    copies = [
        pltpu.make_async_copy(source, target, sems.at[k])
        for k, (source, target) in enumerate(zip(sources, targets))
    ]
    for c in copies:
        c.start()
    m = pos_ref[0]
    rows = own_ref.shape[0]
    copies[0].wait()
    copies[1].wait()
    x = x_ref[...].astype(jnp.float32)
    mean = jnp.mean(x, axis=1, keepdims=True)
    gap = x - mean
    var = jnp.mean(gap * gap, axis=1, keepdims=True)
    normed_ref[...] = (gap * lax.rsqrt(var + EPS) * gain_ref[...]).astype(jnp.bfloat16)

    copies[2].wait()
    copies[3].wait()
    depth = head_ref.shape[0]
    text = text_ref[...]
    part = jnp.where(m == 0, text[:, :depth], text[:, depth:])
    acc_ref[...] = jnp.dot(part, head_ref[...], preferred_element_type=jnp.float32)
    split_rows(acc_ref, m, own_text_ref, other_text_ref)

    copies[4].wait()
    total, block = up_ref.shape[0], 512
    for start in range(0, total, block):
        stop = min(start + block, total)
        acc = lax.dot_general(
            normed_ref[...],
            up_ref[start:stop, :],
            (((1,), (1,)), ((), ())),
            preferred_element_type=jnp.float32,
        )
        hidden_ref[:, start:stop] = jax.nn.gelu(acc, approximate=True).astype(jnp.bfloat16)
    copies[5].wait()
    block = 384
    for start in range(0, acc_ref.shape[1], block):
        acc_ref[:, start : start + block] = jnp.dot(
            hidden_ref[...], down_ref[:, start : start + block], preferred_element_type=jnp.float32
        )
    split_rows(acc_ref, m, own_ref, other_ref)
    x = x_ref[pl.ds(pl.multiple_of(m * rows, rows), rows), :]
    own_ref[...] = own_ref[...] + x.astype(jnp.float32)


def heads(pos, x, gain, text, head, up, down):
    arrays = [x, gain, text, head, up, down]
    rows, width, hidden = x.shape[0], x.shape[1], up.shape[0]
    half, bf16 = rows // 2, jnp.bfloat16
    vmem, hbm = pl.BlockSpec(memory_space=pltpu.VMEM), pl.BlockSpec(memory_space=pl.ANY)
    return pl.pallas_call(
        head_kernel,
        in_specs=[pl.BlockSpec(memory_space=pltpu.SMEM)] + [hbm] * len(arrays),
        out_specs=[vmem] * 4,
        out_shape=[shape((half, width)), shape((half, width), bf16)] * 2,
        scratch_shapes=[pltpu.VMEM(a.shape, a.dtype) for a in arrays]
        + [
            pltpu.VMEM((rows, width), bf16),
            pltpu.VMEM((rows, hidden), bf16),
            pltpu.VMEM((rows, width), jnp.float32),
            pltpu.SemaphoreType.DMA((len(arrays),)),
        ],
        compiler_params=pltpu.CompilerParams(vmem_limit_bytes=52 * 1024 * 1024),
        cost_estimate=pl.CostEstimate(
            flops=4 * rows * width * hidden, bytes_accessed=12 << 20, transcendentals=rows * hidden
        ),
    )(pos, *arrays)


def text_unit_kernel(own_ref, recv_ref, z_ref):
    e = own_ref[...] + recv_ref[...].astype(jnp.float32)
    n = jnp.sqrt(jnp.sum(e * e, axis=1, keepdims=True) + EPS)
    z_ref[...] = (e / n).astype(jnp.bfloat16)


def own_pick(place_row):
    slot = lax.broadcasted_iota(jnp.int32, (CAP, ROWS), 0).astype(jnp.float32)
    return jnp.where(place_row == slot, 1.0, 0.0)


def image_unit_kernel(own_ref, recv_ref, z_ref, unit_ref, n_ref):
    e = own_ref[...] + recv_ref[...].astype(jnp.float32)
    n = jnp.sqrt(jnp.sum(e * e, axis=1, keepdims=True) + EPS)
    unit = e / n
    z_ref[...] = unit.astype(jnp.bfloat16)
    unit_ref[...] = unit
    n_ref[...] = jnp.broadcast_to(n, n_ref.shape)


def sub_unit_kernel(pos_ref, unit_ref, n_ref, place_ref, unit_sub_ref, n_sub_ref):
    pick = own_pick(place_ref[pl.ds(pos_ref[1] * (NX * NY) + pos_ref[4], 1), :])
    unit_sub_ref[...] = jnp.dot(
        pick, unit_ref[...], precision=EXACT, preferred_element_type=jnp.float32
    )
    n_sub = jnp.dot(pick, n_ref[...], precision=EXACT, preferred_element_type=jnp.float32)
    n_sub_ref[...] = jnp.where(n_sub > 0.0, n_sub, 1.0)


def join_kernel(*refs):
    refs[-1][...] = jnp.concatenate([r[...] for r in refs[:-1]], axis=0)


def fold_terms(e):
    n = e.shape[0]
    while n > 1:
        n //= 2
        a, b = e[:n], e[n:]
        e = a + (b + a * b)
    return e[0]


def tile_loss(text, img, own):
    rows, width = text.shape[0], img.shape[0]
    t = lax.dot_general(text, img, (((1,), (1,)), ((), ())), preferred_element_type=jnp.float32)
    t = t * (SCALE * LOG2E) + (BIAS * LOG2E)
    if own:
        row = lax.broadcasted_iota(jnp.int32, (ROWS, width), 0)
        col = lax.broadcasted_iota(jnp.int32, (ROWS, width), 1)
        t = jnp.concatenate([jnp.where(col == row, -t[:ROWS], t[:ROWS]), t[ROWS:]], axis=0)
    t = t.reshape(rows // 8, 8, width)
    high = jnp.sum(jnp.maximum(t, 0.0), axis=0)
    low = jnp.log1p(fold_terms(jnp.exp2(-jnp.abs(t))))
    return high * LN2 + low


def image_row(z, offset):
    return lax.rem(z + (offset + NZ), NZ)


def group_loss(images, pieces, own):
    img = [r[...] for r in images]
    img = img[0] if len(img) == 1 else jnp.concatenate(img, axis=0)
    total = jnp.zeros((8, img.shape[0]), jnp.float32)
    for k, (ref, start) in enumerate(pieces):
        total = total + tile_loss(ref[start : start + BLOCK, :], img, own and k == 0)
    return jnp.sum(total, axis=0, keepdims=True)


def text_pieces(refs):
    return [(ref, start) for ref in refs for start in range(0, ref.shape[0], BLOCK)]


def early_kernel(*refs):
    images, texts, out_ref = refs[: NZ - 1], refs[NZ - 1 : -1], refs[-1]
    pieces = text_pieces(texts)
    for first in range(0, NZ - 1, 2):
        group = images[first : first + 2]
        total = group_loss(group, pieces, first == 0)
        for k in range(len(group)):
            out_ref[first + k : first + k + 1, :] = total[:, k * ROWS : (k + 1) * ROWS]
    out_ref[NZ - 1 :, :] = jnp.zeros((1, ROWS), jnp.float32)


def pair_kernel(pos_ref, chosen_ref, place_ref, early_ref, *refs):
    images, texts, load_ref = refs[:NZ], refs[NZ:-1], refs[-1]
    z, x, y, xy = pos_ref[1], pos_ref[2], pos_ref[3], pos_ref[4]
    planes = NX * NY
    pieces = text_pieces(texts)

    picks = [own_pick(place_ref[pl.ds(image_row(z, o) * planes + xy, 1), :]) for o in ZOFF]
    packed = jnp.concatenate(
        [
            jnp.dot(p.astype(jnp.bfloat16), images[k][...], preferred_element_type=jnp.float32)
            for k, p in enumerate(picks)
        ],
        axis=0,
    ).astype(jnp.bfloat16)

    def text_row(dx, dy):
        tx, ty = lax.rem(x + (dx + NX), NX), lax.rem(y + (dy + NY), NY)
        row = z * planes + tx * NY + lax.rem(ty, 2) * 2 + ty // 2
        return chosen_ref[pl.ds(row, 1), :]

    lines = [text_row(dx, dy) for dx in POFF for dy in POFF]
    total = jnp.zeros(packed.shape, jnp.float32)
    for k, (ref, start) in enumerate(pieces):
        text = ref[start : start + BLOCK, :]
        mask = jnp.concatenate(lines[2 * k : 2 * k + 2], axis=1)
        t = lax.dot_general(
            packed, text, (((1,), (1,)), ((), ())), preferred_element_type=jnp.float32
        )
        t = t * SCALE + BIAS
        sign = jnp.ones(t.shape, jnp.float32)
        if k == 0:
            own = jnp.concatenate([1.0 - 2.0 * picks[0], sign[:CAP, ROWS:]], axis=1)
            sign = jnp.concatenate([own, sign[CAP:]], axis=0)
        t = sign * t
        e = jnp.exp(-jnp.abs(t))
        s = jnp.where(t >= 0, 1.0, e) / (1.0 + e)
        slope = (sign * s * mask).astype(jnp.bfloat16)
        total = total + jnp.dot(slope, text, preferred_element_type=jnp.float32)
    total = total.astype(jnp.bfloat16)
    width = total.shape[1]
    for k, o in enumerate(ZOFF):
        rows = pl.ds(pl.multiple_of(image_row(z, o) * CAP, CAP), CAP)
        load_ref[rows, :width] = total[k * CAP : (k + 1) * CAP, :]

    near, far = text_pieces(texts[:3]), text_pieces(texts[3:])
    late = group_loss(images[NZ - 1 :], near, False)
    for first in range(0, NZ, 2):
        total = group_loss(images[first : first + 2], far, False)
        for k in range(2):
            loss = total[:, k * ROWS : (k + 1) * ROWS]
            loss = loss + (late if first + k == NZ - 1 else early_ref[first + k : first + k + 1, :])
            parts = []
            for _ in range(3):
                part = loss.astype(jnp.bfloat16).astype(jnp.float32)
                loss = loss - part
                parts.append(part)
            parts.append(jnp.zeros((CAP - 3, ROWS), jnp.float32))
            beside = jnp.concatenate(parts, axis=0).astype(jnp.bfloat16)
            row = image_row(z, ZOFF[first + k])
            load_ref[pl.ds(pl.multiple_of(row * CAP, CAP), CAP), width:] = beside


def finish_kernel(load_ref, unit_ref, n_ref, keep_ref, msg_ref):
    width = unit_ref.shape[1]
    cut = width // 2
    total = load_ref[:CAP, :].astype(jnp.float32)
    for z in range(1, NZ):
        total = total + load_ref[z * CAP : (z + 1) * CAP, :].astype(jnp.float32)
    g = SCALE * total[:, :width]
    unit = unit_ref[...]
    grad = (g - unit * jnp.sum(unit * g, axis=1, keepdims=True)) / n_ref[:, :1]
    loss = total[0:1, width:] + total[1:2, width:] + total[2:3, width:]
    line = jnp.concatenate([loss, jnp.zeros((1, cut - ROWS), jnp.float32)], axis=1)
    keep_ref[:CAP, :] = grad[:, cut:]
    keep_ref[CAP:, :] = jnp.broadcast_to(line, (8, cut))
    msg_ref[:CAP, :] = grad[:, :cut]
    msg_ref[CAP:, :] = jnp.broadcast_to(line, (8, cut))


def spread_kernel(pos_ref, keep_ref, recv_ref, place_ref, learn_ref, out_ref):
    learner = pos_ref[5] == 1
    half = jnp.where(learner, keep_ref[:CAP, :], recv_ref[:CAP, :])
    pick = own_pick(place_ref[pl.ds(pos_ref[1] * (NX * NY) + pos_ref[4], 1), :])
    out_ref[...] = lax.dot_general(
        half, pick, (((0,), (0,)), ((), ())), precision=EXACT, preferred_element_type=jnp.float32
    )
    own, other = keep_ref[CAP : CAP + 1, :ROWS], recv_ref[CAP : CAP + 1, :ROWS]
    learn_ref[...] = jnp.where(learner, own - other, other - own)


def shards(image_features, text_features, norm_gain, up_weight, down_weight, text_head, sub_index):
    g_idx = lax.axis_index("grp")
    z_idx = lax.axis_index("z")
    x_idx = lax.axis_index("x")
    m_idx = lax.axis_index("yhi")
    l_idx = lax.axis_index("ylo")
    width = image_features.shape[1]
    rows = image_features.shape[0] // 2
    blocks = NZ * NX * NY
    cut = width // 2
    bf16 = jnp.bfloat16
    pos = [m_idx, z_idx, x_idx, m_idx * 2 + l_idx, (x_idx * 2 + l_idx) * 2 + m_idx, g_idx]
    pos = jnp.stack([p.astype(jnp.int32) for p in pos])
    cells = rows * width

    own_img, other_img, own_text, other_text = heads(
        pos,
        image_features,
        norm_gain,
        text_features,
        text_head[0],
        up_weight[0].T,
        down_weight[0],
    )
    recv_img = over_mp(other_img)
    recv_text = over_mp(other_text)
    chosen, place_of = call(
        index_kernel, [], [sub_index.reshape(1, -1)], [shape((blocks, rows))] * 2, 100 << 20
    )
    z_img, unit, n_img = call(
        image_unit_kernel,
        [],
        [own_img, recv_img],
        [shape((rows, width), bf16), shape((rows, width)), shape((rows, rows))],
        20 * cells,
    )
    own_text, z_img = lax.optimization_barrier((own_text, z_img))
    (z_txt,) = call(
        text_unit_kernel, [], [own_text, recv_text], [shape((rows, width), bf16)], 20 * cells
    )
    line = [z_txt] + [over_plane(z_txt, shift, 0) for shift in (1, -1, 2)]
    back, ahead = [z_img], [z_img]

    def z_step():
        back.append(over_z(back[-1], (1, 1)))
        ahead.append(over_z(ahead[-1], (-1, -1)))

    z_step()
    z_step()
    line[0], back[2], ahead[2] = lax.optimization_barrier((line[0], back[2], ahead[2]))
    (joined,) = call(join_kernel, [], line, [shape((4 * rows, width), bf16)], cells)
    text_back, text_ahead = over_plane(joined, 1, 1), over_plane(joined, -1, 1)
    z_step()
    text_back, text_ahead, back[3], ahead[3] = lax.optimization_barrier(
        (text_back, text_ahead, back[3], ahead[3])
    )
    last = over_z(jnp.where(g_idx == 0, back[3], ahead[3]), (1, -1))
    far_top = over_plane(text_back[: 2 * rows], 1, 1)
    far_low = over_plane(text_ahead[2 * rows :], -1, 1)
    texts = [joined, text_back, text_ahead, far_top, far_low]
    images = [z_img, back[1], ahead[1], back[2], ahead[2], back[3], ahead[3], last]

    all_img, n_text = NZ * rows, NX * NY * rows
    (early,) = call(
        early_kernel,
        [],
        images[:-1] + texts[:3],
        [shape((NZ, rows))],
        all_img * width * n_text,
        transcendentals=all_img * n_text // 2,
    )
    (load,) = call(
        pair_kernel,
        [pos],
        [chosen, place_of, early] + images + texts,
        [shape((NZ * CAP, width + rows), bf16)],
        (all_img + 4 * NZ * CAP) * width * n_text,
        transcendentals=all_img * n_text // 2,
    )
    load = lax.all_to_all(load, "z", 0, 0, tiled=True)
    unit_sub, n_sub = call(
        sub_unit_kernel,
        [pos],
        [unit, n_img, place_of],
        [shape((CAP, width)), shape((CAP, rows))],
        400 * cells,
    )
    keep, msg = call(
        finish_kernel, [], [load, unit_sub, n_sub], [shape((CAP + 8, cut))] * 2, 10 * cells
    )
    learn, image_grad = call(
        spread_kernel,
        [pos],
        [keep, swap_cores(msg), place_of],
        [shape((1, rows)), shape((cut, rows))],
        200 * cells,
    )
    return (learn.reshape(rows), image_grad.T)


def solution(mesh):
    fine = Mesh(mesh.devices.reshape(2, NZ, NX, 2, 2), AXES)
    dp = ("z", "x", "ylo")
    in_specs = (
        P(dp, None),
        P(dp, None),
        P("grp", None),
        P("grp", None, "yhi"),
        P("grp", "yhi", None),
        P("grp", "yhi", None),
        P(),
    )
    out_specs = (P(dp + ("yhi",)), P(dp + ("yhi",), "grp"))
    return jax.shard_map(shards, mesh=fine, in_specs=in_specs, out_specs=out_specs, check_vma=False)
```

```python
import jax
import jax.numpy as jnp
from jax import lax
from jax.experimental import pallas as pl
from jax.experimental.pallas import tpu as pltpu
from jax.sharding import Mesh, PartitionSpec as P

SCALE = 117.0
BIAS = -12.9
EPS = 1e-06
LOG2E = 1.4426950408889634
LN2 = 0.6931471805599453
NZ, NX, NY = 8, 4, 4
ROWS = 128
BLOCK = 256
CAP = 32
AXES = ("grp", "z", "x", "ylo", "yhi")
ZOFF = (0, -1, 1, -2, 2, -3, 3, 4)
POFF = (0, -1, 1, 2)
EXACT = lax.Precision.HIGHEST


def place(g, z, x, y):
    return ((g * NZ + z) * NX + x) * NY + (y % 2) * 2 + y // 2


def permute(v, target, cores=(0, 1)):
    perm = [
        (place(g, z, x, y), place(*target(g, z, x, y)))
        for g in cores
        for z in range(NZ)
        for x in range(NX)
        for y in range(NY)
    ]
    return lax.ppermute(v, AXES, perm)


def over_mp(v):
    return permute(v, lambda g, z, x, y: (g, z, x, (y + 2) % NY))


def over_z(v, shifts, cores=(0, 1)):
    return permute(v, lambda g, z, x, y: (g, (z + shifts[g]) % NZ, x, y), cores)


def over_plane(v, shift, first):
    def target(g, z, x, y):
        if g == first:
            return (g, z, (x + shift) % NX, y)
        return (g, z, x, (y + shift) % NY)

    return permute(v, target)


def swap_cores(v):
    return permute(v, lambda g, z, x, y: (1 - g, z, x, y))


def shape(dims, dtype=jnp.float32):
    return jax.ShapeDtypeStruct(dims, dtype)


def call(kernel, scalars, arrays, outs, flops, mib=8, transcendentals=0, scratch=()):
    vmem = pl.BlockSpec(memory_space=pltpu.VMEM)
    return pl.pallas_call(
        kernel,
        in_specs=[pl.BlockSpec(memory_space=pltpu.SMEM)] * len(scalars) + [vmem] * len(arrays),
        out_specs=[vmem] * len(outs),
        out_shape=outs,
        scratch_shapes=scratch,
        compiler_params=pltpu.CompilerParams(vmem_limit_bytes=mib * 1024 * 1024),
        cost_estimate=pl.CostEstimate(
            flops=flops, bytes_accessed=1 << 20, transcendentals=transcendentals
        ),
    )(*scalars, *arrays)


def index_kernel(sub_ref, chosen_ref, place_ref):
    sub = sub_ref[...]
    line = lax.broadcasted_iota(jnp.int32, (ROWS, sub.shape[1]), 0)
    in_block = jnp.where((sub >> 7) == line, 1.0, 0.0).astype(jnp.bfloat16)
    at_off = jnp.where((sub & 127) == line, 1.0, 0.0).astype(jnp.bfloat16)
    chosen = lax.dot_general(
        in_block, at_off, (((1,), (1,)), ((), ())), preferred_element_type=jnp.float32
    )
    row = lax.broadcasted_iota(jnp.int32, (ROWS, ROWS), 0)
    col = lax.broadcasted_iota(jnp.int32, (ROWS, ROWS), 1)
    upper = jnp.where(row < col, 1.0, 0.0).astype(jnp.bfloat16)
    rank = jnp.dot(chosen.astype(jnp.bfloat16), upper, preferred_element_type=jnp.float32)
    chosen_ref[...] = chosen
    place_ref[...] = jnp.where(chosen > 0.5, rank, -1.0)


def split_rows(acc_ref, m, own_ref, other_ref):
    rows = own_ref.shape[0]
    own_ref[...] = acc_ref[pl.ds(pl.multiple_of(m * rows, rows), rows), :]
    other = acc_ref[pl.ds(pl.multiple_of((1 - m) * rows, rows), rows), :]
    other_ref[...] = other.astype(jnp.bfloat16)


def text_kernel(
    pos_ref, text_hbm, head_hbm, own_ref, other_ref, text_ref, head_ref, acc_ref, sems
):
    copies = [
        pltpu.make_async_copy(text_hbm, text_ref, sems.at[0]),
        pltpu.make_async_copy(head_hbm, head_ref, sems.at[1]),
    ]
    for c in copies:
        c.start()
    for c in copies:
        c.wait()
    depth = head_ref.shape[0]
    m = pos_ref[0]
    text = text_ref[...]
    part = jnp.where(m == 0, text[:, :depth], text[:, depth:])
    acc_ref[...] = jnp.dot(part, head_ref[...], preferred_element_type=jnp.float32)
    split_rows(acc_ref, m, own_ref, other_ref)


def mlp_kernel(
    pos_ref, x_hbm, gain_hbm, up_hbm, down_hbm, own_ref, other_ref,
    x_ref, gain_ref, up_ref, down_ref, normed_ref, hidden_ref, acc_ref, sems,
):
    copies = [
        pltpu.make_async_copy(source, target, sems.at[k])
        for k, (source, target) in enumerate(
            [(x_hbm, x_ref), (gain_hbm, gain_ref), (up_hbm, up_ref), (down_hbm, down_ref)]
        )
    ]
    for c in copies[:3]:
        c.start()
    m = pos_ref[0]
    rows = own_ref.shape[0]
    copies[0].wait()
    copies[1].wait()
    x = x_ref[...].astype(jnp.float32)
    mean = jnp.mean(x, axis=1, keepdims=True)
    gap = x - mean
    var = jnp.mean(gap * gap, axis=1, keepdims=True)
    normed_ref[...] = (gap * lax.rsqrt(var + EPS) * gain_ref[...]).astype(jnp.bfloat16)
    copies[2].wait()
    copies[3].start()
    total, block = up_ref.shape[0], 512
    for start in range(0, total, block):
        stop = min(start + block, total)
        acc = lax.dot_general(
            normed_ref[...],
            up_ref[start:stop, :],
            (((1,), (1,)), ((), ())),
            preferred_element_type=jnp.float32,
        )
        hidden_ref[:, start:stop] = jax.nn.gelu(acc, approximate=True).astype(jnp.bfloat16)
    copies[3].wait()
    block = 384
    for start in range(0, acc_ref.shape[1], block):
        acc_ref[:, start : start + block] = jnp.dot(
            hidden_ref[...], down_ref[:, start : start + block], preferred_element_type=jnp.float32
        )
    split_rows(acc_ref, m, own_ref, other_ref)
    x = x_ref[pl.ds(pl.multiple_of(m * rows, rows), rows), :]
    own_ref[...] = own_ref[...] + x.astype(jnp.float32)


def from_hbm(kernel, pos, arrays, rows, width, scratch, flops):
    vmem, hbm = pl.BlockSpec(memory_space=pltpu.VMEM), pl.BlockSpec(memory_space=pl.ANY)
    return pl.pallas_call(
        kernel,
        in_specs=[pl.BlockSpec(memory_space=pltpu.SMEM)] + [hbm] * len(arrays),
        out_specs=[vmem, vmem],
        out_shape=[shape((rows, width)), shape((rows, width), jnp.bfloat16)],
        scratch_shapes=[pltpu.VMEM(a.shape, a.dtype) for a in arrays]
        + scratch
        + [pltpu.VMEM((2 * rows, width), jnp.float32), pltpu.SemaphoreType.DMA((len(arrays),))],
        compiler_params=pltpu.CompilerParams(vmem_limit_bytes=52 * 1024 * 1024),
        cost_estimate=pl.CostEstimate(flops=flops, bytes_accessed=11 << 20, transcendentals=0),
    )(pos, *arrays)


def text_unit_kernel(own_ref, recv_ref, z_ref):
    e = own_ref[...] + recv_ref[...].astype(jnp.float32)
    n = jnp.sqrt(jnp.sum(e * e, axis=1, keepdims=True) + EPS)
    z_ref[...] = (e / n).astype(jnp.bfloat16)


def own_pick(place_row):
    slot = lax.broadcasted_iota(jnp.int32, (CAP, ROWS), 0).astype(jnp.float32)
    return jnp.where(place_row == slot, 1.0, 0.0)


def image_unit_kernel(own_ref, recv_ref, z_ref, unit_ref, n_ref):
    e = own_ref[...] + recv_ref[...].astype(jnp.float32)
    n = jnp.sqrt(jnp.sum(e * e, axis=1, keepdims=True) + EPS)
    unit = e / n
    z_ref[...] = unit.astype(jnp.bfloat16)
    unit_ref[...] = unit
    n_ref[...] = jnp.broadcast_to(n, n_ref.shape)


def sub_unit_kernel(pos_ref, unit_ref, n_ref, place_ref, unit_sub_ref, n_sub_ref):
    pick = own_pick(place_ref[pl.ds(pos_ref[1] * (NX * NY) + pos_ref[4], 1), :])
    unit_sub_ref[...] = jnp.dot(
        pick, unit_ref[...], precision=EXACT, preferred_element_type=jnp.float32
    )
    n_sub = jnp.dot(pick, n_ref[...], precision=EXACT, preferred_element_type=jnp.float32)
    n_sub_ref[...] = jnp.where(n_sub > 0.0, n_sub, 1.0)


def join_kernel(*refs):
    refs[-1][...] = jnp.concatenate([r[...] for r in refs[:-1]], axis=0)


def fold_terms(e):
    n = e.shape[0]
    while n > 1:
        n //= 2
        a, b = e[:n], e[n:]
        e = a + (b + a * b)
    return e[0]


def tile_loss(text, img, own):
    rows, width = text.shape[0], img.shape[0]
    t = lax.dot_general(text, img, (((1,), (1,)), ((), ())), preferred_element_type=jnp.float32)
    t = t * (SCALE * LOG2E) + (BIAS * LOG2E)
    if own:
        row = lax.broadcasted_iota(jnp.int32, (ROWS, width), 0)
        col = lax.broadcasted_iota(jnp.int32, (ROWS, width), 1)
        t = jnp.concatenate([jnp.where(col == row, -t[:ROWS], t[:ROWS]), t[ROWS:]], axis=0)
    t = t.reshape(rows // 8, 8, width)
    high = jnp.sum(jnp.maximum(t, 0.0), axis=0)
    low = jnp.log1p(fold_terms(jnp.exp2(-jnp.abs(t))))
    return high * LN2 + low


def image_row(z, offset):
    return lax.rem(z + (offset + NZ), NZ)


def group_loss(images, pieces, own):
    img = [r[...] for r in images]
    img = img[0] if len(img) == 1 else jnp.concatenate(img, axis=0)
    total = jnp.zeros((8, img.shape[0]), jnp.float32)
    for k, (ref, start) in enumerate(pieces):
        total = total + tile_loss(ref[start : start + BLOCK, :], img, own and k == 0)
    return jnp.sum(total, axis=0, keepdims=True)


def text_pieces(refs):
    return [(ref, start) for ref in refs for start in range(0, ref.shape[0], BLOCK)]


def early_kernel(*refs):
    images, texts, out_ref = refs[: NZ - 1], refs[NZ - 1 : -1], refs[-1]
    pieces = text_pieces(texts)
    for first in range(0, NZ - 1, 2):
        group = images[first : first + 2]
        total = group_loss(group, pieces, first == 0)
        for k in range(len(group)):
            out_ref[first + k : first + k + 1, :] = total[:, k * ROWS : (k + 1) * ROWS]
    out_ref[NZ - 1 :, :] = jnp.zeros((1, ROWS), jnp.float32)


def pair_kernel(pos_ref, chosen_ref, place_ref, early_ref, *refs):
    images, texts, load_ref = refs[:NZ], refs[NZ:-1], refs[-1]
    z, x, y, xy = pos_ref[1], pos_ref[2], pos_ref[3], pos_ref[4]
    planes = NX * NY
    pieces = text_pieces(texts)

    picks = [own_pick(place_ref[pl.ds(image_row(z, o) * planes + xy, 1), :]) for o in ZOFF]
    packed = jnp.concatenate(
        [
            jnp.dot(p.astype(jnp.bfloat16), images[k][...], preferred_element_type=jnp.float32)
            for k, p in enumerate(picks)
        ],
        axis=0,
    ).astype(jnp.bfloat16)

    def text_row(dx, dy):
        tx, ty = lax.rem(x + (dx + NX), NX), lax.rem(y + (dy + NY), NY)
        row = z * planes + tx * NY + lax.rem(ty, 2) * 2 + ty // 2
        return chosen_ref[pl.ds(row, 1), :]

    lines = [text_row(dx, dy) for dx in POFF for dy in POFF]
    total = jnp.zeros(packed.shape, jnp.float32)
    for k, (ref, start) in enumerate(pieces):
        text = ref[start : start + BLOCK, :]
        mask = jnp.concatenate(lines[2 * k : 2 * k + 2], axis=1)
        t = lax.dot_general(
            packed, text, (((1,), (1,)), ((), ())), preferred_element_type=jnp.float32
        )
        t = t * SCALE + BIAS
        sign = jnp.ones(t.shape, jnp.float32)
        if k == 0:
            own = jnp.concatenate([1.0 - 2.0 * picks[0], sign[:CAP, ROWS:]], axis=1)
            sign = jnp.concatenate([own, sign[CAP:]], axis=0)
        t = sign * t
        e = jnp.exp(-jnp.abs(t))
        s = jnp.where(t >= 0, 1.0, e) / (1.0 + e)
        slope = (sign * s * mask).astype(jnp.bfloat16)
        total = total + jnp.dot(slope, text, preferred_element_type=jnp.float32)
    total = total.astype(jnp.bfloat16)
    width = total.shape[1]
    for k, o in enumerate(ZOFF):
        rows = pl.ds(pl.multiple_of(image_row(z, o) * CAP, CAP), CAP)
        load_ref[rows, :width] = total[k * CAP : (k + 1) * CAP, :]

    near, far = text_pieces(texts[:3]), text_pieces(texts[3:])
    late = group_loss(images[NZ - 1 :], near, False)
    for first in range(0, NZ, 2):
        total = group_loss(images[first : first + 2], far, False)
        for k in range(2):
            loss = total[:, k * ROWS : (k + 1) * ROWS]
            loss = loss + (late if first + k == NZ - 1 else early_ref[first + k : first + k + 1, :])
            parts = []
            for _ in range(3):
                part = loss.astype(jnp.bfloat16).astype(jnp.float32)
                loss = loss - part
                parts.append(part)
            parts.append(jnp.zeros((CAP - 3, ROWS), jnp.float32))
            beside = jnp.concatenate(parts, axis=0).astype(jnp.bfloat16)
            row = image_row(z, ZOFF[first + k])
            load_ref[pl.ds(pl.multiple_of(row * CAP, CAP), CAP), width:] = beside


def finish_kernel(load_ref, unit_ref, n_ref, keep_ref, msg_ref):
    width = unit_ref.shape[1]
    cut = width // 2
    total = load_ref[:CAP, :].astype(jnp.float32)
    for z in range(1, NZ):
        total = total + load_ref[z * CAP : (z + 1) * CAP, :].astype(jnp.float32)
    g = SCALE * total[:, :width]
    unit = unit_ref[...]
    grad = (g - unit * jnp.sum(unit * g, axis=1, keepdims=True)) / n_ref[:, :1]
    loss = total[0:1, width:] + total[1:2, width:] + total[2:3, width:]
    line = jnp.concatenate([loss, jnp.zeros((1, cut - ROWS), jnp.float32)], axis=1)
    keep_ref[:CAP, :] = grad[:, cut:]
    keep_ref[CAP:, :] = jnp.broadcast_to(line, (8, cut))
    msg_ref[:CAP, :] = grad[:, :cut]
    msg_ref[CAP:, :] = jnp.broadcast_to(line, (8, cut))


def spread_kernel(pos_ref, keep_ref, recv_ref, place_ref, learn_ref, out_ref):
    learner = pos_ref[5] == 1
    half = jnp.where(learner, keep_ref[:CAP, :], recv_ref[:CAP, :])
    pick = own_pick(place_ref[pl.ds(pos_ref[1] * (NX * NY) + pos_ref[4], 1), :])
    out_ref[...] = lax.dot_general(
        half, pick, (((0,), (0,)), ((), ())), precision=EXACT, preferred_element_type=jnp.float32
    )
    own, other = keep_ref[CAP : CAP + 1, :ROWS], recv_ref[CAP : CAP + 1, :ROWS]
    learn_ref[...] = jnp.where(learner, own - other, other - own)


def shards(image_features, text_features, norm_gain, up_weight, down_weight, text_head, sub_index):
    g_idx = lax.axis_index("grp")
    z_idx = lax.axis_index("z")
    x_idx = lax.axis_index("x")
    m_idx = lax.axis_index("yhi")
    l_idx = lax.axis_index("ylo")
    width = image_features.shape[1]
    rows = image_features.shape[0] // 2
    blocks = NZ * NX * NY
    cut = width // 2
    bf16 = jnp.bfloat16
    pos = [m_idx, z_idx, x_idx, m_idx * 2 + l_idx, (x_idx * 2 + l_idx) * 2 + m_idx, g_idx]
    pos = jnp.stack([p.astype(jnp.int32) for p in pos])
    cells = rows * width

    own_text, other_text = from_hbm(
        text_kernel, pos, [text_features, text_head[0]], rows, width, [], 2 * cells * width
    )
    recv_text = over_mp(other_text)
    features, own_text = lax.optimization_barrier((image_features, own_text))
    hidden = up_weight.shape[2]
    own_img, other_img = from_hbm(
        mlp_kernel,
        pos,
        [features, norm_gain, up_weight[0].T, down_weight[0]],
        rows,
        width,
        [pltpu.VMEM((2 * rows, width), bf16), pltpu.VMEM((2 * rows, hidden), bf16)],
        8 * cells * hidden,
    )
    other_img, recv_text = lax.optimization_barrier((other_img, recv_text))
    recv_img = over_mp(other_img)
    chosen, place_of = call(
        index_kernel, [], [sub_index.reshape(1, -1)], [shape((blocks, rows))] * 2, 100 << 20
    )
    z_img, unit, n_img = call(
        image_unit_kernel,
        [],
        [own_img, recv_img],
        [shape((rows, width), bf16), shape((rows, width)), shape((rows, rows))],
        20 * cells,
    )
    (z_txt,) = call(
        text_unit_kernel, [], [own_text, recv_text], [shape((rows, width), bf16)], 20 * cells
    )
    line = [z_txt] + [over_plane(z_txt, shift, 0) for shift in (1, -1, 2)]
    z_img, *line = lax.optimization_barrier((z_img, *line))
    back, ahead = [z_img], [z_img]

    def z_step():
        back.append(over_z(back[-1], (1, 1)))
        ahead.append(over_z(ahead[-1], (-1, -1)))

    (joined,) = call(join_kernel, [], line, [shape((4 * rows, width), bf16)], cells)
    text_back, text_ahead = over_plane(joined, 1, 1), over_plane(joined, -1, 1)
    for _ in range(3):
        z_step()
    last = over_z(jnp.where(g_idx == 0, back[3], ahead[3]), (1, -1))
    far_top = over_plane(text_back[: 2 * rows], 1, 1)
    far_low = over_plane(text_ahead[2 * rows :], -1, 1)
    texts = [joined, text_back, text_ahead, far_top, far_low]
    images = [z_img, back[1], ahead[1], back[2], ahead[2], back[3], ahead[3], last]

    all_img, n_text = NZ * rows, NX * NY * rows
    (early,) = call(
        early_kernel,
        [],
        images[:-1] + texts[:3],
        [shape((NZ, rows))],
        all_img * width * n_text,
        transcendentals=all_img * n_text // 2,
    )
    (load,) = call(
        pair_kernel,
        [pos],
        [chosen, place_of, early] + images + texts,
        [shape((NZ * CAP, width + rows), bf16)],
        (all_img + 4 * NZ * CAP) * width * n_text,
        transcendentals=all_img * n_text // 2,
    )
    load = lax.all_to_all(load, "z", 0, 0, tiled=True)
    unit_sub, n_sub = call(
        sub_unit_kernel,
        [pos],
        [unit, n_img, place_of],
        [shape((CAP, width)), shape((CAP, rows))],
        400 * cells,
    )
    keep, msg = call(
        finish_kernel, [], [load, unit_sub, n_sub], [shape((CAP + 8, cut))] * 2, 10 * cells
    )
    learn, image_grad = call(
        spread_kernel,
        [pos],
        [keep, swap_cores(msg), place_of],
        [shape((1, rows)), shape((cut, rows))],
        200 * cells,
    )
    return (learn.reshape(rows), image_grad.T)


def solution(mesh):
    fine = Mesh(mesh.devices.reshape(2, NZ, NX, 2, 2), AXES)
    dp = ("z", "x", "ylo")
    in_specs = (
        P(dp, None),
        P(dp, None),
        P("grp", None),
        P("grp", None, "yhi"),
        P("grp", "yhi", None),
        P("grp", "yhi", None),
        P(),
    )
    out_specs = (P(dp + ("yhi",)), P(dp + ("yhi",), "grp"))
    return jax.shard_map(shards, mesh=fine, in_specs=in_specs, out_specs=out_specs, check_vma=False)
```

```python
import jax
import jax.numpy as jnp
from jax import lax
from jax.experimental import pallas as pl
from jax.experimental.pallas import tpu as pltpu
from jax.sharding import Mesh, PartitionSpec as P

SCALE = 117.0
BIAS = -12.9
EPS = 1e-06
LOG2E = 1.4426950408889634
LN2 = 0.6931471805599453
NZ, NX, NY = 8, 4, 4
ROWS = 128
CAP = 32
AXES = ("grp", "z", "x", "ylo", "yhi")
ZOFF = (0, -1, 1, -2, 2, -3, 3, 4)
POFF = (0, -1, 1, 2)
EXACT = lax.Precision.HIGHEST


def place(g, z, x, y):
    return ((g * NZ + z) * NX + x) * NY + (y % 2) * 2 + y // 2


def permute(v, target, cores=(0, 1)):
    perm = [
        (place(g, z, x, y), place(*target(g, z, x, y)))
        for g in cores
        for z in range(NZ)
        for x in range(NX)
        for y in range(NY)
    ]
    return lax.ppermute(v, AXES, perm)


def over_mp(v):
    return permute(v, lambda g, z, x, y: (g, z, x, (y + 2) % NY))


def over_z(v, shifts, cores=(0, 1)):
    return permute(v, lambda g, z, x, y: (g, (z + shifts[g]) % NZ, x, y), cores)


def over_plane(v, shift, first):
    def target(g, z, x, y):
        if g == first:
            return (g, z, (x + shift) % NX, y)
        return (g, z, x, (y + shift) % NY)

    return permute(v, target)


def swap_cores(v):
    return permute(v, lambda g, z, x, y: (1 - g, z, x, y))


def shape(dims, dtype=jnp.float32):
    return jax.ShapeDtypeStruct(dims, dtype)


def call(kernel, scalars, arrays, outs, flops, mib=8, transcendentals=0, scratch=()):
    vmem = pl.BlockSpec(memory_space=pltpu.VMEM)
    return pl.pallas_call(
        kernel,
        in_specs=[pl.BlockSpec(memory_space=pltpu.SMEM)] * len(scalars) + [vmem] * len(arrays),
        out_specs=[vmem] * len(outs),
        out_shape=outs,
        scratch_shapes=scratch,
        compiler_params=pltpu.CompilerParams(vmem_limit_bytes=mib * 1024 * 1024),
        cost_estimate=pl.CostEstimate(
            flops=flops, bytes_accessed=1 << 20, transcendentals=transcendentals
        ),
    )(*scalars, *arrays)


def index_kernel(sub_ref, chosen_ref, place_ref):
    sub = sub_ref[...]
    line = lax.broadcasted_iota(jnp.int32, (ROWS, sub.shape[1]), 0)
    in_block = jnp.where((sub >> 7) == line, 1.0, 0.0).astype(jnp.bfloat16)
    at_off = jnp.where((sub & 127) == line, 1.0, 0.0).astype(jnp.bfloat16)
    chosen = lax.dot_general(
        in_block, at_off, (((1,), (1,)), ((), ())), preferred_element_type=jnp.float32
    )
    row = lax.broadcasted_iota(jnp.int32, (ROWS, ROWS), 0)
    col = lax.broadcasted_iota(jnp.int32, (ROWS, ROWS), 1)
    upper = jnp.where(row < col, 1.0, 0.0).astype(jnp.bfloat16)
    rank = jnp.dot(chosen.astype(jnp.bfloat16), upper, preferred_element_type=jnp.float32)
    chosen_ref[...] = chosen
    place_ref[...] = jnp.where(chosen > 0.5, rank, -1.0)


def split_rows(acc_ref, m, own_ref, other_ref):
    rows = own_ref.shape[0]
    own_ref[...] = acc_ref[pl.ds(pl.multiple_of(m * rows, rows), rows), :]
    other = acc_ref[pl.ds(pl.multiple_of((1 - m) * rows, rows), rows), :]
    other_ref[...] = other.astype(jnp.bfloat16)


def text_kernel(
    pos_ref, text_hbm, head_hbm, own_ref, other_ref, text_ref, head_ref, acc_ref, sems
):
    copies = [
        pltpu.make_async_copy(text_hbm, text_ref, sems.at[0]),
        pltpu.make_async_copy(head_hbm, head_ref, sems.at[1]),
    ]
    for c in copies:
        c.start()
    for c in copies:
        c.wait()
    depth = head_ref.shape[0]
    m = pos_ref[0]
    text = text_ref[...]
    part = jnp.where(m == 0, text[:, :depth], text[:, depth:])
    acc_ref[...] = jnp.dot(part, head_ref[...], preferred_element_type=jnp.float32)
    split_rows(acc_ref, m, own_ref, other_ref)


def mlp_kernel(
    pos_ref, x_hbm, gain_hbm, up_hbm, down_hbm, own_ref, other_ref,
    x_ref, gain_ref, up_ref, down_ref, normed_ref, hidden_ref, acc_ref, sems,
):
    copies = [
        pltpu.make_async_copy(source, target, sems.at[k])
        for k, (source, target) in enumerate(
            [(x_hbm, x_ref), (gain_hbm, gain_ref), (up_hbm, up_ref), (down_hbm, down_ref)]
        )
    ]
    for c in copies[:3]:
        c.start()
    m = pos_ref[0]
    rows = own_ref.shape[0]
    copies[0].wait()
    copies[1].wait()
    x = x_ref[...].astype(jnp.float32)
    mean = jnp.mean(x, axis=1, keepdims=True)
    gap = x - mean
    var = jnp.mean(gap * gap, axis=1, keepdims=True)
    normed_ref[...] = (gap * lax.rsqrt(var + EPS) * gain_ref[...]).astype(jnp.bfloat16)
    copies[2].wait()
    copies[3].start()
    total, block = up_ref.shape[0], 512
    for start in range(0, total, block):
        stop = min(start + block, total)
        acc = lax.dot_general(
            normed_ref[...],
            up_ref[start:stop, :],
            (((1,), (1,)), ((), ())),
            preferred_element_type=jnp.float32,
        )
        hidden_ref[:, start:stop] = jax.nn.gelu(acc, approximate=True).astype(jnp.bfloat16)
    copies[3].wait()
    block = 384
    for start in range(0, acc_ref.shape[1], block):
        acc_ref[:, start : start + block] = jnp.dot(
            hidden_ref[...], down_ref[:, start : start + block], preferred_element_type=jnp.float32
        )
    split_rows(acc_ref, m, own_ref, other_ref)
    x = x_ref[pl.ds(pl.multiple_of(m * rows, rows), rows), :]
    own_ref[...] = own_ref[...] + x.astype(jnp.float32)


def from_hbm(kernel, pos, arrays, rows, width, scratch, flops):
    vmem, hbm = pl.BlockSpec(memory_space=pltpu.VMEM), pl.BlockSpec(memory_space=pl.ANY)
    return pl.pallas_call(
        kernel,
        in_specs=[pl.BlockSpec(memory_space=pltpu.SMEM)] + [hbm] * len(arrays),
        out_specs=[vmem, vmem],
        out_shape=[shape((rows, width)), shape((rows, width), jnp.bfloat16)],
        scratch_shapes=[pltpu.VMEM(a.shape, a.dtype) for a in arrays]
        + scratch
        + [pltpu.VMEM((2 * rows, width), jnp.float32), pltpu.SemaphoreType.DMA((len(arrays),))],
        compiler_params=pltpu.CompilerParams(vmem_limit_bytes=52 * 1024 * 1024),
        cost_estimate=pl.CostEstimate(flops=flops, bytes_accessed=11 << 20, transcendentals=0),
    )(pos, *arrays)


def text_unit_kernel(own_ref, recv_ref, z_ref):
    e = own_ref[...] + recv_ref[...].astype(jnp.float32)
    n = jnp.sqrt(jnp.sum(e * e, axis=1, keepdims=True) + EPS)
    z_ref[...] = (e / n).astype(jnp.bfloat16)


def own_pick(place_row):
    slot = lax.broadcasted_iota(jnp.int32, (CAP, ROWS), 0).astype(jnp.float32)
    return jnp.where(place_row == slot, 1.0, 0.0)


def image_unit_kernel(own_ref, recv_ref, z_ref, unit_ref, n_ref):
    e = own_ref[...] + recv_ref[...].astype(jnp.float32)
    n = jnp.sqrt(jnp.sum(e * e, axis=1, keepdims=True) + EPS)
    unit = e / n
    z_ref[...] = unit.astype(jnp.bfloat16)
    unit_ref[...] = unit
    n_ref[...] = jnp.broadcast_to(n, n_ref.shape)


def sub_unit_kernel(pos_ref, unit_ref, n_ref, place_ref, unit_sub_ref, n_sub_ref):
    pick = own_pick(place_ref[pl.ds(pos_ref[1] * (NX * NY) + pos_ref[4], 1), :])
    unit_sub_ref[...] = jnp.dot(
        pick, unit_ref[...], precision=EXACT, preferred_element_type=jnp.float32
    )
    n_sub = jnp.dot(pick, n_ref[...], precision=EXACT, preferred_element_type=jnp.float32)
    n_sub_ref[...] = jnp.where(n_sub > 0.0, n_sub, 1.0)


def join_kernel(*refs):
    refs[-1][...] = jnp.concatenate([r[...] for r in refs[:-1]], axis=0)


def fold_terms(e):
    n = e.shape[0]
    while n > 1:
        n //= 2
        a, b = e[:n], e[n:]
        e = a + (b + a * b)
    return e[0]


def tile_loss(text, img, own):
    rows, width = text.shape[0], img.shape[0]
    t = lax.dot_general(text, img, (((1,), (1,)), ((), ())), preferred_element_type=jnp.float32)
    t = t * (SCALE * LOG2E) + (BIAS * LOG2E)
    if own:
        row = lax.broadcasted_iota(jnp.int32, (ROWS, width), 0)
        col = lax.broadcasted_iota(jnp.int32, (ROWS, width), 1)
        t = jnp.concatenate([jnp.where(col == row, -t[:ROWS], t[:ROWS]), t[ROWS:]], axis=0)
    t = t.reshape(rows // 8, 8, width)
    high = jnp.sum(jnp.maximum(t, 0.0), axis=0)
    low = jnp.log1p(fold_terms(jnp.exp2(-jnp.abs(t))))
    return high * LN2 + low


def image_row(z, offset):
    return lax.rem(z + (offset + NZ), NZ)


def group_loss(images, texts, own):
    img = [r[...] for r in images]
    img = img[0] if len(img) == 1 else jnp.concatenate(img, axis=0)
    total = jnp.zeros((8, img.shape[0]), jnp.float32)
    for k, ref in enumerate(texts):
        total = total + tile_loss(ref[...], img, own and k == 0)
    return jnp.sum(total, axis=0, keepdims=True)


def early_kernel(*refs):
    images, texts, out_ref = refs[: NZ - 1], refs[NZ - 1 : -1], refs[-1]
    for first in range(0, NZ - 1, 2):
        group = images[first : first + 2]
        total = group_loss(group, texts, first == 0)
        for k in range(len(group)):
            out_ref[first + k : first + k + 1, :] = total[:, k * ROWS : (k + 1) * ROWS]
    out_ref[NZ - 1 :, :] = jnp.zeros((1, ROWS), jnp.float32)


def pair_kernel(pos_ref, chosen_ref, place_ref, early_ref, *refs):
    images, texts, load_ref = refs[:NZ], refs[NZ:-1], refs[-1]
    z, x, y, xy = pos_ref[1], pos_ref[2], pos_ref[3], pos_ref[4]
    planes = NX * NY

    picks = [own_pick(place_ref[pl.ds(image_row(z, o) * planes + xy, 1), :]) for o in ZOFF]
    packed = jnp.concatenate(
        [
            jnp.dot(p.astype(jnp.bfloat16), images[k][...], preferred_element_type=jnp.float32)
            for k, p in enumerate(picks)
        ],
        axis=0,
    ).astype(jnp.bfloat16)

    def text_row(dx, dy):
        tx, ty = lax.rem(x + (dx + NX), NX), lax.rem(y + (dy + NY), NY)
        row = z * planes + tx * NY + lax.rem(ty, 2) * 2 + ty // 2
        return chosen_ref[pl.ds(row, 1), :]

    lines = [text_row(dx, dy) for dx in POFF for dy in POFF]
    total = jnp.zeros(packed.shape, jnp.float32)
    for k, ref in enumerate(texts):
        text = ref[...]
        count = text.shape[0] // ROWS
        mask = jnp.concatenate(lines[:count], axis=1)
        lines = lines[count:]
        t = lax.dot_general(
            packed, text, (((1,), (1,)), ((), ())), preferred_element_type=jnp.float32
        )
        t = t * SCALE + BIAS
        sign = jnp.ones(t.shape, jnp.float32)
        if k == 0:
            own = jnp.concatenate([1.0 - 2.0 * picks[0], sign[:CAP, ROWS:]], axis=1)
            sign = jnp.concatenate([own, sign[CAP:]], axis=0)
        t = sign * t
        e = jnp.exp(-jnp.abs(t))
        s = jnp.where(t >= 0, 1.0, e) / (1.0 + e)
        slope = (sign * s * mask).astype(jnp.bfloat16)
        total = total + jnp.dot(slope, text, preferred_element_type=jnp.float32)
    total = total.astype(jnp.bfloat16)
    width = total.shape[1]
    for k, o in enumerate(ZOFF):
        rows = pl.ds(pl.multiple_of(image_row(z, o) * CAP, CAP), CAP)
        load_ref[rows, :width] = total[k * CAP : (k + 1) * CAP, :]

    near, far = texts[:3], texts[3:]
    late = group_loss(images[NZ - 1 :], near, False)
    for first in range(0, NZ, 2):
        total = group_loss(images[first : first + 2], far, False)
        for k in range(2):
            loss = total[:, k * ROWS : (k + 1) * ROWS]
            loss = loss + (late if first + k == NZ - 1 else early_ref[first + k : first + k + 1, :])
            parts = []
            for _ in range(3):
                part = loss.astype(jnp.bfloat16).astype(jnp.float32)
                loss = loss - part
                parts.append(part)
            parts.append(jnp.zeros((CAP - 3, ROWS), jnp.float32))
            beside = jnp.concatenate(parts, axis=0).astype(jnp.bfloat16)
            row = image_row(z, ZOFF[first + k])
            load_ref[pl.ds(pl.multiple_of(row * CAP, CAP), CAP), width:] = beside


def finish_kernel(load_ref, unit_ref, n_ref, keep_ref, msg_ref):
    width = unit_ref.shape[1]
    cut = width // 2
    total = load_ref[:CAP, :].astype(jnp.float32)
    for z in range(1, NZ):
        total = total + load_ref[z * CAP : (z + 1) * CAP, :].astype(jnp.float32)
    g = SCALE * total[:, :width]
    unit = unit_ref[...]
    grad = (g - unit * jnp.sum(unit * g, axis=1, keepdims=True)) / n_ref[:, :1]
    loss = total[0:1, width:] + total[1:2, width:] + total[2:3, width:]
    line = jnp.concatenate([loss, jnp.zeros((1, cut - ROWS), jnp.float32)], axis=1)
    keep_ref[:CAP, :] = grad[:, cut:]
    keep_ref[CAP:, :] = jnp.broadcast_to(line, (8, cut))
    msg_ref[:CAP, :] = grad[:, :cut]
    msg_ref[CAP:, :] = jnp.broadcast_to(line, (8, cut))


def spread_kernel(pos_ref, keep_ref, recv_ref, place_ref, learn_ref, out_ref):
    learner = pos_ref[5] == 1
    half = jnp.where(learner, keep_ref[:CAP, :], recv_ref[:CAP, :])
    pick = own_pick(place_ref[pl.ds(pos_ref[1] * (NX * NY) + pos_ref[4], 1), :])
    out_ref[...] = lax.dot_general(
        half, pick, (((0,), (0,)), ((), ())), precision=EXACT, preferred_element_type=jnp.float32
    )
    own, other = keep_ref[CAP : CAP + 1, :ROWS], recv_ref[CAP : CAP + 1, :ROWS]
    learn_ref[...] = jnp.where(learner, own - other, other - own)


def shards(image_features, text_features, norm_gain, up_weight, down_weight, text_head, sub_index):
    g_idx = lax.axis_index("grp")
    z_idx = lax.axis_index("z")
    x_idx = lax.axis_index("x")
    m_idx = lax.axis_index("yhi")
    l_idx = lax.axis_index("ylo")
    width = image_features.shape[1]
    rows = image_features.shape[0] // 2
    blocks = NZ * NX * NY
    cut = width // 2
    bf16 = jnp.bfloat16
    pos = [m_idx, z_idx, x_idx, m_idx * 2 + l_idx, (x_idx * 2 + l_idx) * 2 + m_idx, g_idx]
    pos = jnp.stack([p.astype(jnp.int32) for p in pos])
    cells = rows * width

    own_text, other_text = from_hbm(
        text_kernel, pos, [text_features, text_head[0]], rows, width, [], 2 * cells * width
    )
    recv_text = over_mp(other_text)
    features, own_text = lax.optimization_barrier((image_features, own_text))
    hidden = up_weight.shape[2]
    own_img, other_img = from_hbm(
        mlp_kernel,
        pos,
        [features, norm_gain, up_weight[0].T, down_weight[0]],
        rows,
        width,
        [pltpu.VMEM((2 * rows, width), bf16), pltpu.VMEM((2 * rows, hidden), bf16)],
        8 * cells * hidden,
    )
    other_img, recv_text = lax.optimization_barrier((other_img, recv_text))
    recv_img = over_mp(other_img)
    chosen, place_of = call(
        index_kernel, [], [sub_index.reshape(1, -1)], [shape((blocks, rows))] * 2, 100 << 20
    )
    z_img, unit, n_img = call(
        image_unit_kernel,
        [],
        [own_img, recv_img],
        [shape((rows, width), bf16), shape((rows, width)), shape((rows, rows))],
        20 * cells,
    )
    (z_txt,) = call(
        text_unit_kernel, [], [own_text, recv_text], [shape((rows, width), bf16)], 20 * cells
    )
    line = [z_txt] + [over_plane(z_txt, shift, 0) for shift in (1, -1, 2)]
    z_img, line[3] = lax.optimization_barrier((z_img, line[3]))
    back, ahead = [z_img], [z_img]

    def z_step():
        back.append(over_z(back[-1], (1, 1)))
        ahead.append(over_z(ahead[-1], (-1, -1)))

    z_step()
    line[0], back[1], ahead[1] = lax.optimization_barrier((line[0], back[1], ahead[1]))
    (joined,) = call(join_kernel, [], line, [shape((4 * rows, width), bf16)], cells)
    text_back, text_ahead = over_plane(joined, 1, 1), over_plane(joined, -1, 1)
    z_step()
    z_step()
    last = over_z(jnp.where(g_idx == 0, back[3], ahead[3]), (1, -1))
    far_top = over_plane(text_back[: 2 * rows], 1, 1)
    far_low = over_plane(text_ahead[2 * rows :], -1, 1)
    texts = [joined, text_back, text_ahead, far_top, far_low]
    images = [z_img, back[1], ahead[1], back[2], ahead[2], back[3], ahead[3], last]

    all_img, n_text = NZ * rows, NX * NY * rows
    (early,) = call(
        early_kernel,
        [],
        images[:-1] + texts[:3],
        [shape((NZ, rows))],
        all_img * width * n_text,
        transcendentals=all_img * n_text // 2,
    )
    (load,) = call(
        pair_kernel,
        [pos],
        [chosen, place_of, early] + images + texts,
        [shape((NZ * CAP, width + rows), bf16)],
        (all_img + 4 * NZ * CAP) * width * n_text,
        transcendentals=all_img * n_text // 2,
    )
    load = lax.all_to_all(load, "z", 0, 0, tiled=True)
    unit_sub, n_sub = call(
        sub_unit_kernel,
        [pos],
        [unit, n_img, place_of],
        [shape((CAP, width)), shape((CAP, rows))],
        400 * cells,
    )
    keep, msg = call(
        finish_kernel, [], [load, unit_sub, n_sub], [shape((CAP + 8, cut))] * 2, 10 * cells
    )
    learn, image_grad = call(
        spread_kernel,
        [pos],
        [keep, swap_cores(msg), place_of],
        [shape((1, rows)), shape((cut, rows))],
        200 * cells,
    )
    return (learn.reshape(rows), image_grad.T)


def solution(mesh):
    fine = Mesh(mesh.devices.reshape(2, NZ, NX, 2, 2), AXES)
    dp = ("z", "x", "ylo")
    in_specs = (
        P(dp, None),
        P(dp, None),
        P("grp", None),
        P("grp", None, "yhi"),
        P("grp", "yhi", None),
        P("grp", "yhi", None),
        P(),
    )
    out_specs = (P(dp + ("yhi",)), P(dp + ("yhi",), "grp"))
    return jax.shard_map(shards, mesh=fine, in_specs=in_specs, out_specs=out_specs, check_vma=False)
```

```python
import jax
import jax.numpy as jnp
from jax import lax
from jax.experimental import pallas as pl
from jax.experimental.pallas import tpu as pltpu
from jax.sharding import Mesh, PartitionSpec as P

SCALE = 117.0
BIAS = -12.9
EPS = 1e-06
LOG2E = 1.4426950408889634
LN2 = 0.6931471805599453
NZ, NX, NY = 8, 4, 4
ROWS = 128
CAP = 32
AXES = ("grp", "z", "x", "ylo", "yhi")
ZOFF = (0, -1, 1, -2, 2, -3, 3, 4)
POFF = (0, -1, 1, 2)
EXACT = lax.Precision.HIGHEST


def place(g, z, x, y):
    return ((g * NZ + z) * NX + x) * NY + (y % 2) * 2 + y // 2


def permute(v, target, cores=(0, 1)):
    perm = [
        (place(g, z, x, y), place(*target(g, z, x, y)))
        for g in cores
        for z in range(NZ)
        for x in range(NX)
        for y in range(NY)
    ]
    return lax.ppermute(v, AXES, perm)


def over_mp(v):
    return permute(v, lambda g, z, x, y: (g, z, x, (y + 2) % NY))


def over_z(v, shifts, cores=(0, 1)):
    return permute(v, lambda g, z, x, y: (g, (z + shifts[g]) % NZ, x, y), cores)


def over_plane(v, shift, first):
    def target(g, z, x, y):
        if g == first:
            return (g, z, (x + shift) % NX, y)
        return (g, z, x, (y + shift) % NY)

    return permute(v, target)


def swap_cores(v):
    return permute(v, lambda g, z, x, y: (1 - g, z, x, y))


def shape(dims, dtype=jnp.float32):
    return jax.ShapeDtypeStruct(dims, dtype)


def call(kernel, scalars, arrays, outs, flops, mib=8, transcendentals=0, scratch=()):
    vmem = pl.BlockSpec(memory_space=pltpu.VMEM)
    return pl.pallas_call(
        kernel,
        in_specs=[pl.BlockSpec(memory_space=pltpu.SMEM)] * len(scalars) + [vmem] * len(arrays),
        out_specs=[vmem] * len(outs),
        out_shape=outs,
        scratch_shapes=scratch,
        compiler_params=pltpu.CompilerParams(vmem_limit_bytes=mib * 1024 * 1024),
        cost_estimate=pl.CostEstimate(
            flops=flops, bytes_accessed=1 << 20, transcendentals=transcendentals
        ),
    )(*scalars, *arrays)


def index_kernel(sub_ref, chosen_ref, place_ref):
    sub = sub_ref[...]
    line = lax.broadcasted_iota(jnp.int32, (ROWS, sub.shape[1]), 0)
    in_block = jnp.where((sub >> 7) == line, 1.0, 0.0).astype(jnp.bfloat16)
    at_off = jnp.where((sub & 127) == line, 1.0, 0.0).astype(jnp.bfloat16)
    chosen = lax.dot_general(
        in_block, at_off, (((1,), (1,)), ((), ())), preferred_element_type=jnp.float32
    )
    row = lax.broadcasted_iota(jnp.int32, (ROWS, ROWS), 0)
    col = lax.broadcasted_iota(jnp.int32, (ROWS, ROWS), 1)
    upper = jnp.where(row < col, 1.0, 0.0).astype(jnp.bfloat16)
    rank = jnp.dot(chosen.astype(jnp.bfloat16), upper, preferred_element_type=jnp.float32)
    chosen_ref[...] = chosen
    place_ref[...] = jnp.where(chosen > 0.5, rank, -1.0)


def split_rows(acc_ref, m, own_ref, other_ref):
    rows = own_ref.shape[0]
    own_ref[...] = acc_ref[pl.ds(pl.multiple_of(m * rows, rows), rows), :]
    other = acc_ref[pl.ds(pl.multiple_of((1 - m) * rows, rows), rows), :]
    other_ref[...] = other.astype(jnp.bfloat16)


def text_kernel(
    pos_ref, text_hbm, head_hbm, own_ref, other_ref, text_ref, head_ref, acc_ref, sems
):
    copies = [
        pltpu.make_async_copy(text_hbm, text_ref, sems.at[0]),
        pltpu.make_async_copy(head_hbm, head_ref, sems.at[1]),
    ]
    for c in copies:
        c.start()
    for c in copies:
        c.wait()
    depth = head_ref.shape[0]
    m = pos_ref[0]
    text = text_ref[...]
    part = jnp.where(m == 0, text[:, :depth], text[:, depth:])
    acc_ref[...] = jnp.dot(part, head_ref[...], preferred_element_type=jnp.float32)
    split_rows(acc_ref, m, own_ref, other_ref)


def mlp_kernel(
    pos_ref, x_hbm, gain_hbm, up_hbm, down_hbm, own_ref, other_ref,
    x_ref, gain_ref, up_ref, down_ref, normed_ref, hidden_ref, acc_ref, sems,
):
    copies = [
        pltpu.make_async_copy(source, target, sems.at[k])
        for k, (source, target) in enumerate(
            [(x_hbm, x_ref), (gain_hbm, gain_ref), (up_hbm, up_ref), (down_hbm, down_ref)]
        )
    ]
    for c in copies[:3]:
        c.start()
    m = pos_ref[0]
    rows = own_ref.shape[0]
    copies[0].wait()
    copies[1].wait()
    x = x_ref[...].astype(jnp.float32)
    mean = jnp.mean(x, axis=1, keepdims=True)
    gap = x - mean
    var = jnp.mean(gap * gap, axis=1, keepdims=True)
    normed_ref[...] = (gap * lax.rsqrt(var + EPS) * gain_ref[...]).astype(jnp.bfloat16)
    copies[2].wait()
    copies[3].start()
    total, block = up_ref.shape[0], 512
    for start in range(0, total, block):
        stop = min(start + block, total)
        acc = lax.dot_general(
            normed_ref[...],
            up_ref[start:stop, :],
            (((1,), (1,)), ((), ())),
            preferred_element_type=jnp.float32,
        )
        hidden_ref[:, start:stop] = jax.nn.gelu(acc, approximate=True).astype(jnp.bfloat16)
    copies[3].wait()
    block = 384
    for start in range(0, acc_ref.shape[1], block):
        acc_ref[:, start : start + block] = jnp.dot(
            hidden_ref[...], down_ref[:, start : start + block], preferred_element_type=jnp.float32
        )
    split_rows(acc_ref, m, own_ref, other_ref)
    x = x_ref[pl.ds(pl.multiple_of(m * rows, rows), rows), :]
    own_ref[...] = own_ref[...] + x.astype(jnp.float32)


def from_hbm(kernel, pos, arrays, rows, width, scratch, flops):
    vmem, hbm = pl.BlockSpec(memory_space=pltpu.VMEM), pl.BlockSpec(memory_space=pl.ANY)
    return pl.pallas_call(
        kernel,
        in_specs=[pl.BlockSpec(memory_space=pltpu.SMEM)] + [hbm] * len(arrays),
        out_specs=[vmem, vmem],
        out_shape=[shape((rows, width)), shape((rows, width), jnp.bfloat16)],
        scratch_shapes=[pltpu.VMEM(a.shape, a.dtype) for a in arrays]
        + scratch
        + [pltpu.VMEM((2 * rows, width), jnp.float32), pltpu.SemaphoreType.DMA((len(arrays),))],
        compiler_params=pltpu.CompilerParams(vmem_limit_bytes=52 * 1024 * 1024),
        cost_estimate=pl.CostEstimate(flops=flops, bytes_accessed=11 << 20, transcendentals=0),
    )(pos, *arrays)


def text_unit_kernel(own_ref, recv_ref, z_ref):
    e = own_ref[...] + recv_ref[...].astype(jnp.float32)
    n = jnp.sqrt(jnp.sum(e * e, axis=1, keepdims=True) + EPS)
    z_ref[...] = (e / n).astype(jnp.bfloat16)


def own_pick(place_row):
    slot = lax.broadcasted_iota(jnp.int32, (CAP, ROWS), 0).astype(jnp.float32)
    return jnp.where(place_row == slot, 1.0, 0.0)


def image_unit_kernel(own_ref, recv_ref, z_ref, unit_ref, n_ref):
    e = own_ref[...] + recv_ref[...].astype(jnp.float32)
    n = jnp.sqrt(jnp.sum(e * e, axis=1, keepdims=True) + EPS)
    unit = e / n
    z_ref[...] = unit.astype(jnp.bfloat16)
    unit_ref[...] = unit
    n_ref[...] = jnp.broadcast_to(n, n_ref.shape)


def sub_unit_kernel(pos_ref, unit_ref, n_ref, place_ref, unit_sub_ref, n_sub_ref):
    pick = own_pick(place_ref[pl.ds(pos_ref[1] * (NX * NY) + pos_ref[4], 1), :])
    unit_sub_ref[...] = jnp.dot(
        pick, unit_ref[...], precision=EXACT, preferred_element_type=jnp.float32
    )
    n_sub = jnp.dot(pick, n_ref[...], precision=EXACT, preferred_element_type=jnp.float32)
    n_sub_ref[...] = jnp.where(n_sub > 0.0, n_sub, 1.0)


def join_kernel(*refs):
    refs[-1][...] = jnp.concatenate([r[...] for r in refs[:-1]], axis=0)


def fold_terms(e):
    n = e.shape[0]
    while n > 1:
        n //= 2
        a, b = e[:n], e[n:]
        e = a + (b + a * b)
    return e[0]


def tile_dot(text, img):
    return lax.dot_general(text, img, (((1,), (1,)), ((), ())), preferred_element_type=jnp.float32)


def tile_loss(d, own):
    rows, width = d.shape
    d = d + BIAS / SCALE
    if own:
        row = lax.broadcasted_iota(jnp.int32, (ROWS, width), 0)
        col = lax.broadcasted_iota(jnp.int32, (ROWS, width), 1)
        d = jnp.concatenate([jnp.where(col == row, -d[:ROWS], d[:ROWS]), d[ROWS:]], axis=0)
    d = d.reshape(rows // 8, 8, width)
    high = jnp.sum(jnp.maximum(d, 0.0), axis=0)
    low = jnp.log1p(fold_terms(jnp.exp2(jnp.abs(d) * (-SCALE * LOG2E))))
    return high * SCALE + low


def losses_of(tasks):
    totals = [jnp.zeros((8, sum(r.shape[0] for r in g)), jnp.float32) for g, _, _ in tasks]
    waiting = None
    for number, (group, texts, own) in enumerate(tasks):
        img = [r[...] for r in group]
        img = img[0] if len(img) == 1 else jnp.concatenate(img, axis=0)
        for k, ref in enumerate(texts):
            d = tile_dot(ref[...], img)
            if waiting is not None:
                before, tile, diagonal = waiting
                totals[before] = totals[before] + tile_loss(tile, diagonal)
            waiting = (number, d, own and k == 0)
    before, tile, diagonal = waiting
    totals[before] = totals[before] + tile_loss(tile, diagonal)
    return [jnp.sum(t, axis=0, keepdims=True) for t in totals]


def image_row(z, offset):
    return lax.rem(z + (offset + NZ), NZ)


def early_kernel(*refs):
    images, texts, out_ref = refs[: NZ - 1], refs[NZ - 1 : -1], refs[-1]
    tasks = [(images[k : k + 2], texts, k == 0) for k in range(0, NZ - 1, 2)]
    for number, total in enumerate(losses_of(tasks)):
        for k in range(total.shape[1] // ROWS):
            row = 2 * number + k
            out_ref[row : row + 1, :] = total[:, k * ROWS : (k + 1) * ROWS]
    out_ref[NZ - 1 :, :] = jnp.zeros((1, ROWS), jnp.float32)


def pair_kernel(pos_ref, chosen_ref, place_ref, early_ref, *refs):
    images, texts, load_ref = refs[:NZ], refs[NZ:-1], refs[-1]
    z, x, y, xy = pos_ref[1], pos_ref[2], pos_ref[3], pos_ref[4]
    planes = NX * NY

    picks = [own_pick(place_ref[pl.ds(image_row(z, o) * planes + xy, 1), :]) for o in ZOFF]
    packed = jnp.concatenate(
        [
            jnp.dot(p.astype(jnp.bfloat16), images[k][...], preferred_element_type=jnp.float32)
            for k, p in enumerate(picks)
        ],
        axis=0,
    ).astype(jnp.bfloat16)

    def text_row(dx, dy):
        tx, ty = lax.rem(x + (dx + NX), NX), lax.rem(y + (dy + NY), NY)
        row = z * planes + tx * NY + lax.rem(ty, 2) * 2 + ty // 2
        return chosen_ref[pl.ds(row, 1), :]

    lines = [text_row(dx, dy) for dx in POFF for dy in POFF]
    total = jnp.zeros(packed.shape, jnp.float32)
    ahead = tile_dot(packed, texts[0][...])
    for k, ref in enumerate(texts):
        text = ref[...]
        t = ahead * SCALE + BIAS
        if k + 1 < len(texts):
            ahead = tile_dot(packed, texts[k + 1][...])
        count = text.shape[0] // ROWS
        mask = jnp.concatenate(lines[:count], axis=1)
        lines = lines[count:]
        sign = jnp.ones(t.shape, jnp.float32)
        if k == 0:
            own = jnp.concatenate([1.0 - 2.0 * picks[0], sign[:CAP, ROWS:]], axis=1)
            sign = jnp.concatenate([own, sign[CAP:]], axis=0)
            t = sign * t
        e = jnp.exp(-jnp.abs(t))
        s = jnp.where(t >= 0, 1.0, e) / (1.0 + e)
        slope = (s * (sign * mask) if k == 0 else s * mask).astype(jnp.bfloat16)
        total = total + jnp.dot(slope, text, preferred_element_type=jnp.float32)
    total = total.astype(jnp.bfloat16)
    width = total.shape[1]
    for k, o in enumerate(ZOFF):
        rows = pl.ds(pl.multiple_of(image_row(z, o) * CAP, CAP), CAP)
        load_ref[rows, :width] = total[k * CAP : (k + 1) * CAP, :]

    near, far = texts[:3], texts[3:]
    tasks = [(images[k : k + 2], far, False) for k in range(0, NZ, 2)]
    *totals, late = losses_of(tasks + [(images[NZ - 1 :], near, False)])
    for first, total in zip(range(0, NZ, 2), totals):
        for k in range(2):
            loss = total[:, k * ROWS : (k + 1) * ROWS]
            loss = loss + (late if first + k == NZ - 1 else early_ref[first + k : first + k + 1, :])
            parts = []
            for _ in range(3):
                part = loss.astype(jnp.bfloat16).astype(jnp.float32)
                loss = loss - part
                parts.append(part)
            parts.append(jnp.zeros((CAP - 3, ROWS), jnp.float32))
            beside = jnp.concatenate(parts, axis=0).astype(jnp.bfloat16)
            row = image_row(z, ZOFF[first + k])
            load_ref[pl.ds(pl.multiple_of(row * CAP, CAP), CAP), width:] = beside


def finish_kernel(load_ref, unit_ref, n_ref, keep_ref, msg_ref):
    width = unit_ref.shape[1]
    cut = width // 2
    total = load_ref[:CAP, :].astype(jnp.float32)
    for z in range(1, NZ):
        total = total + load_ref[z * CAP : (z + 1) * CAP, :].astype(jnp.float32)
    g = SCALE * total[:, :width]
    unit = unit_ref[...]
    grad = (g - unit * jnp.sum(unit * g, axis=1, keepdims=True)) / n_ref[:, :1]
    loss = total[0:1, width:] + total[1:2, width:] + total[2:3, width:]
    line = jnp.concatenate([loss, jnp.zeros((1, cut - ROWS), jnp.float32)], axis=1)
    keep_ref[:CAP, :] = grad[:, cut:]
    keep_ref[CAP:, :] = jnp.broadcast_to(line, (8, cut))
    msg_ref[:CAP, :] = grad[:, :cut]
    msg_ref[CAP:, :] = jnp.broadcast_to(line, (8, cut))


def spread_kernel(pos_ref, keep_ref, recv_ref, place_ref, learn_ref, out_ref):
    learner = pos_ref[5] == 1
    half = jnp.where(learner, keep_ref[:CAP, :], recv_ref[:CAP, :])
    pick = own_pick(place_ref[pl.ds(pos_ref[1] * (NX * NY) + pos_ref[4], 1), :])
    out_ref[...] = lax.dot_general(
        half, pick, (((0,), (0,)), ((), ())), precision=EXACT, preferred_element_type=jnp.float32
    )
    own, other = keep_ref[CAP : CAP + 1, :ROWS], recv_ref[CAP : CAP + 1, :ROWS]
    learn_ref[...] = jnp.where(learner, own - other, other - own)


def shards(image_features, text_features, norm_gain, up_weight, down_weight, text_head, sub_index):
    g_idx = lax.axis_index("grp")
    z_idx = lax.axis_index("z")
    x_idx = lax.axis_index("x")
    m_idx = lax.axis_index("yhi")
    l_idx = lax.axis_index("ylo")
    width = image_features.shape[1]
    rows = image_features.shape[0] // 2
    blocks = NZ * NX * NY
    cut = width // 2
    bf16 = jnp.bfloat16
    pos = [m_idx, z_idx, x_idx, m_idx * 2 + l_idx, (x_idx * 2 + l_idx) * 2 + m_idx, g_idx]
    pos = jnp.stack([p.astype(jnp.int32) for p in pos])
    cells = rows * width

    own_text, other_text = from_hbm(
        text_kernel, pos, [text_features, text_head[0]], rows, width, [], 2 * cells * width
    )
    recv_text = over_mp(other_text)
    features, own_text = lax.optimization_barrier((image_features, own_text))
    hidden = up_weight.shape[2]
    own_img, other_img = from_hbm(
        mlp_kernel,
        pos,
        [features, norm_gain, up_weight[0].T, down_weight[0]],
        rows,
        width,
        [pltpu.VMEM((2 * rows, width), bf16), pltpu.VMEM((2 * rows, hidden), bf16)],
        8 * cells * hidden,
    )
    other_img, recv_text = lax.optimization_barrier((other_img, recv_text))
    recv_img = over_mp(other_img)
    chosen, place_of = call(
        index_kernel, [], [sub_index.reshape(1, -1)], [shape((blocks, rows))] * 2, 100 << 20
    )
    own_img, place_of, chosen = lax.optimization_barrier((own_img, place_of, chosen))
    z_img, unit, n_img = call(
        image_unit_kernel,
        [],
        [own_img, recv_img],
        [shape((rows, width), bf16), shape((rows, width)), shape((rows, rows))],
        20 * cells,
    )
    (z_txt,) = call(
        text_unit_kernel, [], [own_text, recv_text], [shape((rows, width), bf16)], 20 * cells
    )
    line = [z_txt] + [over_plane(z_txt, shift, 0) for shift in (1, -1, 2)]
    z_img, line[1], line[2] = lax.optimization_barrier((z_img, line[1], line[2]))
    back, ahead = [z_img], [z_img]

    def z_step():
        back.append(over_z(back[-1], (1, 1)))
        ahead.append(over_z(ahead[-1], (-1, -1)))

    z_step()
    line[0], back[1], ahead[1] = lax.optimization_barrier((line[0], back[1], ahead[1]))
    (joined,) = call(join_kernel, [], line, [shape((4 * rows, width), bf16)], cells)
    text_back, text_ahead = over_plane(joined, 1, 1), over_plane(joined, -1, 1)
    z_step()
    z_step()
    last = over_z(jnp.where(g_idx == 0, back[3], ahead[3]), (1, -1))
    far_top = over_plane(text_back[: 2 * rows], 1, 1)
    far_low = over_plane(text_ahead[2 * rows :], -1, 1)
    texts = [joined, text_back, text_ahead, far_top, far_low]
    images = [z_img, back[1], ahead[1], back[2], ahead[2], back[3], ahead[3], last]

    all_img, n_text = NZ * rows, NX * NY * rows
    (early,) = call(
        early_kernel,
        [],
        images[:-1] + texts[:3],
        [shape((NZ, rows))],
        all_img * width * n_text,
        transcendentals=all_img * n_text // 2,
    )
    (load,) = call(
        pair_kernel,
        [pos],
        [chosen, place_of, early] + images + texts,
        [shape((NZ * CAP, width + rows), bf16)],
        (all_img + 4 * NZ * CAP) * width * n_text,
        transcendentals=all_img * n_text // 2,
    )
    load = lax.all_to_all(load, "z", 0, 0, tiled=True)
    unit_sub, n_sub = call(
        sub_unit_kernel,
        [pos],
        [unit, n_img, place_of],
        [shape((CAP, width)), shape((CAP, rows))],
        400 * cells,
    )
    keep, msg = call(
        finish_kernel, [], [load, unit_sub, n_sub], [shape((CAP + 8, cut))] * 2, 10 * cells
    )
    learn, image_grad = call(
        spread_kernel,
        [pos],
        [keep, swap_cores(msg), place_of],
        [shape((1, rows)), shape((cut, rows))],
        200 * cells,
    )
    return (learn.reshape(rows), image_grad.T)


def solution(mesh):
    fine = Mesh(mesh.devices.reshape(2, NZ, NX, 2, 2), AXES)
    dp = ("z", "x", "ylo")
    in_specs = (
        P(dp, None),
        P(dp, None),
        P("grp", None),
        P("grp", None, "yhi"),
        P("grp", "yhi", None),
        P("grp", "yhi", None),
        P(),
    )
    out_specs = (P(dp + ("yhi",)), P(dp + ("yhi",), "grp"))
    return jax.shard_map(shards, mesh=fine, in_specs=in_specs, out_specs=out_specs, check_vma=False)
```

```python
import jax
import jax.numpy as jnp
from jax import lax
from jax.experimental import pallas as pl
from jax.experimental.pallas import tpu as pltpu
from jax.sharding import Mesh, PartitionSpec as P

SCALE = 117.0
BIAS = -12.9
EPS = 1e-06
LOG2E = 1.4426950408889634
LN2 = 0.6931471805599453
NZ, NX, NY = 8, 4, 4
ROWS = 128
CAP = 32
AXES = ("grp", "z", "x", "ylo", "yhi")
ZOFF = (0, -1, 1, -2, 2, -3, 3, 4)
POFF = (0, -1, 1, 2)
EXACT = lax.Precision.HIGHEST


def place(g, z, x, y):
    return ((g * NZ + z) * NX + x) * NY + (y % 2) * 2 + y // 2


def permute(v, target, cores=(0, 1)):
    perm = [
        (place(g, z, x, y), place(*target(g, z, x, y)))
        for g in cores
        for z in range(NZ)
        for x in range(NX)
        for y in range(NY)
    ]
    return lax.ppermute(v, AXES, perm)


def over_mp(v):
    return permute(v, lambda g, z, x, y: (g, z, x, (y + 2) % NY))


def over_z(v, shifts, cores=(0, 1)):
    return permute(v, lambda g, z, x, y: (g, (z + shifts[g]) % NZ, x, y), cores)


def over_plane(v, shift, first):
    def target(g, z, x, y):
        if g == first:
            return (g, z, (x + shift) % NX, y)
        return (g, z, x, (y + shift) % NY)

    return permute(v, target)


def swap_cores(v):
    return permute(v, lambda g, z, x, y: (1 - g, z, x, y))


def shape(dims, dtype=jnp.float32):
    return jax.ShapeDtypeStruct(dims, dtype)


def call(kernel, scalars, arrays, outs, flops, mib=8, transcendentals=0, scratch=()):
    vmem = pl.BlockSpec(memory_space=pltpu.VMEM)
    return pl.pallas_call(
        kernel,
        in_specs=[pl.BlockSpec(memory_space=pltpu.SMEM)] * len(scalars) + [vmem] * len(arrays),
        out_specs=[vmem] * len(outs),
        out_shape=outs,
        scratch_shapes=scratch,
        compiler_params=pltpu.CompilerParams(vmem_limit_bytes=mib * 1024 * 1024),
        cost_estimate=pl.CostEstimate(
            flops=flops, bytes_accessed=1 << 20, transcendentals=transcendentals
        ),
    )(*scalars, *arrays)


def index_kernel(sub_ref, chosen_ref, place_ref):
    sub = sub_ref[...]
    line = lax.broadcasted_iota(jnp.int32, (ROWS, sub.shape[1]), 0)
    in_block = jnp.where((sub >> 7) == line, 1.0, 0.0).astype(jnp.bfloat16)
    at_off = jnp.where((sub & 127) == line, 1.0, 0.0).astype(jnp.bfloat16)
    chosen = lax.dot_general(
        in_block, at_off, (((1,), (1,)), ((), ())), preferred_element_type=jnp.float32
    )
    row = lax.broadcasted_iota(jnp.int32, (ROWS, ROWS), 0)
    col = lax.broadcasted_iota(jnp.int32, (ROWS, ROWS), 1)
    upper = jnp.where(row < col, 1.0, 0.0).astype(jnp.bfloat16)
    rank = jnp.dot(chosen.astype(jnp.bfloat16), upper, preferred_element_type=jnp.float32)
    chosen_ref[...] = chosen
    place_ref[...] = jnp.where(chosen > 0.5, rank, -1.0)


def split_rows(acc_ref, m, own_ref, other_ref):
    rows = own_ref.shape[0]
    own_ref[...] = acc_ref[pl.ds(pl.multiple_of(m * rows, rows), rows), :]
    other = acc_ref[pl.ds(pl.multiple_of((1 - m) * rows, rows), rows), :]
    other_ref[...] = other.astype(jnp.bfloat16)


def front_kernel(
    pos_ref, x_hbm, gain_hbm, text_hbm, head_hbm,
    own_ref, other_ref, normed_ref, own_x_ref,
    x_ref, gain_ref, text_ref, head_ref, acc_ref, sems,
):
    copies = [
        pltpu.make_async_copy(source, target, sems.at[k])
        for k, (source, target) in enumerate(
            [(x_hbm, x_ref), (gain_hbm, gain_ref), (text_hbm, text_ref), (head_hbm, head_ref)]
        )
    ]
    for c in copies:
        c.start()
    m = pos_ref[0]
    rows = own_ref.shape[0]
    copies[0].wait()
    copies[1].wait()
    x = x_ref[...].astype(jnp.float32)
    mean = jnp.mean(x, axis=1, keepdims=True)
    gap = x - mean
    var = jnp.mean(gap * gap, axis=1, keepdims=True)
    normed_ref[...] = (gap * lax.rsqrt(var + EPS) * gain_ref[...]).astype(jnp.bfloat16)
    own_x_ref[...] = x_ref[pl.ds(pl.multiple_of(m * rows, rows), rows), :]
    copies[2].wait()
    copies[3].wait()
    depth = head_ref.shape[0]
    text = text_ref[...]
    part = jnp.where(m == 0, text[:, :depth], text[:, depth:])
    acc_ref[...] = jnp.dot(part, head_ref[...], preferred_element_type=jnp.float32)
    split_rows(acc_ref, m, own_ref, other_ref)


def front(pos, x, gain, text, head):
    arrays = [x, gain, text, head]
    rows, width = x.shape
    half, bf16 = rows // 2, jnp.bfloat16
    vmem, hbm = pl.BlockSpec(memory_space=pltpu.VMEM), pl.BlockSpec(memory_space=pl.ANY)
    return pl.pallas_call(
        front_kernel,
        in_specs=[pl.BlockSpec(memory_space=pltpu.SMEM)] + [hbm] * len(arrays),
        out_specs=[vmem] * 4,
        out_shape=[
            shape((half, width)),
            shape((half, width), bf16),
            shape((rows, width), bf16),
            shape((half, width), bf16),
        ],
        scratch_shapes=[pltpu.VMEM(a.shape, a.dtype) for a in arrays]
        + [pltpu.VMEM((rows, width), jnp.float32), pltpu.SemaphoreType.DMA((len(arrays),))],
        compiler_params=pltpu.CompilerParams(vmem_limit_bytes=52 * 1024 * 1024),
        cost_estimate=pl.CostEstimate(
            flops=2 * rows * width * head.shape[0], bytes_accessed=4 << 20, transcendentals=0
        ),
    )(pos, *arrays)


def mlp_kernel(
    pos_ref, normed_ref, own_x_ref, up_hbm, down_hbm, own_ref, other_ref,
    up_ref, down_ref, hidden_ref, acc_ref, sems,
):
    first = pltpu.make_async_copy(up_hbm, up_ref, sems.at[0])
    second = pltpu.make_async_copy(down_hbm, down_ref, sems.at[1])
    first.start()
    first.wait()
    second.start()
    total, block = up_ref.shape[0], 512
    for start in range(0, total, block):
        stop = min(start + block, total)
        acc = lax.dot_general(
            normed_ref[...],
            up_ref[start:stop, :],
            (((1,), (1,)), ((), ())),
            preferred_element_type=jnp.float32,
        )
        hidden_ref[:, start:stop] = jax.nn.gelu(acc, approximate=True).astype(jnp.bfloat16)
    second.wait()
    block = 384
    for start in range(0, acc_ref.shape[1], block):
        acc_ref[:, start : start + block] = jnp.dot(
            hidden_ref[...], down_ref[:, start : start + block], preferred_element_type=jnp.float32
        )
    split_rows(acc_ref, pos_ref[0], own_ref, other_ref)
    own_ref[...] = own_ref[...] + own_x_ref[...].astype(jnp.float32)


def image_mlp(pos, normed, own_x, up, down):
    rows, width = normed.shape
    half, hidden, bf16 = rows // 2, up.shape[0], jnp.bfloat16
    vmem, hbm = pl.BlockSpec(memory_space=pltpu.VMEM), pl.BlockSpec(memory_space=pl.ANY)
    return pl.pallas_call(
        mlp_kernel,
        in_specs=[pl.BlockSpec(memory_space=pltpu.SMEM), vmem, vmem, hbm, hbm],
        out_specs=[vmem, vmem],
        out_shape=[shape((half, width)), shape((half, width), bf16)],
        scratch_shapes=[
            pltpu.VMEM(up.shape, bf16),
            pltpu.VMEM(down.shape, bf16),
            pltpu.VMEM((rows, hidden), bf16),
            pltpu.VMEM((rows, width), jnp.float32),
            pltpu.SemaphoreType.DMA((2,)),
        ],
        compiler_params=pltpu.CompilerParams(vmem_limit_bytes=52 * 1024 * 1024),
        cost_estimate=pl.CostEstimate(
            flops=4 * rows * width * hidden, bytes_accessed=11 << 20, transcendentals=rows * hidden
        ),
    )(pos, normed, own_x, up, down)


def text_unit_kernel(own_ref, recv_ref, z_ref):
    e = own_ref[...] + recv_ref[...].astype(jnp.float32)
    n = jnp.sqrt(jnp.sum(e * e, axis=1, keepdims=True) + EPS)
    z_ref[...] = (e / n).astype(jnp.bfloat16)


def own_pick(place_row):
    slot = lax.broadcasted_iota(jnp.int32, (CAP, ROWS), 0).astype(jnp.float32)
    return jnp.where(place_row == slot, 1.0, 0.0)


def image_unit_kernel(own_ref, recv_ref, z_ref, unit_ref, n_ref):
    e = own_ref[...] + recv_ref[...].astype(jnp.float32)
    n = jnp.sqrt(jnp.sum(e * e, axis=1, keepdims=True) + EPS)
    unit = e / n
    z_ref[...] = unit.astype(jnp.bfloat16)
    unit_ref[...] = unit
    n_ref[...] = jnp.broadcast_to(n, n_ref.shape)


def sub_unit_kernel(pos_ref, unit_ref, n_ref, place_ref, unit_sub_ref, n_sub_ref):
    pick = own_pick(place_ref[pl.ds(pos_ref[1] * (NX * NY) + pos_ref[4], 1), :])
    unit_sub_ref[...] = jnp.dot(
        pick, unit_ref[...], precision=EXACT, preferred_element_type=jnp.float32
    )
    n_sub = jnp.dot(pick, n_ref[...], precision=EXACT, preferred_element_type=jnp.float32)
    n_sub_ref[...] = jnp.where(n_sub > 0.0, n_sub, 1.0)


def join_kernel(*refs):
    refs[-1][...] = jnp.concatenate([r[...] for r in refs[:-1]], axis=0)


def fold_terms(e):
    n = e.shape[0]
    while n > 1:
        n //= 2
        a, b = e[:n], e[n:]
        e = a + (b + a * b)
    return e[0]


def tile_dot(text, img):
    return lax.dot_general(text, img, (((1,), (1,)), ((), ())), preferred_element_type=jnp.float32)


def tile_loss(d, own):
    rows, width = d.shape
    d = d + BIAS / SCALE
    if own:
        row = lax.broadcasted_iota(jnp.int32, (ROWS, width), 0)
        col = lax.broadcasted_iota(jnp.int32, (ROWS, width), 1)
        d = jnp.concatenate([jnp.where(col == row, -d[:ROWS], d[:ROWS]), d[ROWS:]], axis=0)
    d = d.reshape(rows // 8, 8, width)
    high = jnp.sum(jnp.maximum(d, 0.0), axis=0)
    low = jnp.log1p(fold_terms(jnp.exp2(jnp.abs(d) * (-SCALE * LOG2E))))
    return high * SCALE + low


def losses_of(tasks):
    totals = [jnp.zeros((8, sum(r.shape[0] for r in g)), jnp.float32) for g, _, _ in tasks]
    waiting = None
    for number, (group, texts, own) in enumerate(tasks):
        img = [r[...] for r in group]
        img = img[0] if len(img) == 1 else jnp.concatenate(img, axis=0)
        for k, ref in enumerate(texts):
            d = tile_dot(ref[...], img)
            if waiting is not None:
                before, tile, diagonal = waiting
                totals[before] = totals[before] + tile_loss(tile, diagonal)
            waiting = (number, d, own and k == 0)
    before, tile, diagonal = waiting
    totals[before] = totals[before] + tile_loss(tile, diagonal)
    return [jnp.sum(t, axis=0, keepdims=True) for t in totals]


def image_row(z, offset):
    return lax.rem(z + (offset + NZ), NZ)


def early_kernel(*refs):
    images, texts, out_ref = refs[: NZ - 1], refs[NZ - 1 : -1], refs[-1]
    tasks = [(images[k : k + 2], texts, k == 0) for k in range(0, NZ - 1, 2)]
    for number, total in enumerate(losses_of(tasks)):
        for k in range(total.shape[1] // ROWS):
            row = 2 * number + k
            out_ref[row : row + 1, :] = total[:, k * ROWS : (k + 1) * ROWS]
    out_ref[NZ - 1 :, :] = jnp.zeros((1, ROWS), jnp.float32)


def pair_kernel(pos_ref, chosen_ref, place_ref, early_ref, *refs):
    images, texts, load_ref = refs[:NZ], refs[NZ:-1], refs[-1]
    z, x, y, xy = pos_ref[1], pos_ref[2], pos_ref[3], pos_ref[4]
    planes = NX * NY

    picks = [own_pick(place_ref[pl.ds(image_row(z, o) * planes + xy, 1), :]) for o in ZOFF]
    packed = jnp.concatenate(
        [
            jnp.dot(p.astype(jnp.bfloat16), images[k][...], preferred_element_type=jnp.float32)
            for k, p in enumerate(picks)
        ],
        axis=0,
    ).astype(jnp.bfloat16)

    def text_row(dx, dy):
        tx, ty = lax.rem(x + (dx + NX), NX), lax.rem(y + (dy + NY), NY)
        row = z * planes + tx * NY + lax.rem(ty, 2) * 2 + ty // 2
        return chosen_ref[pl.ds(row, 1), :]

    lines = [text_row(dx, dy) for dx in POFF for dy in POFF]
    total = jnp.zeros(packed.shape, jnp.float32)
    ahead = tile_dot(packed, texts[0][...])
    for k, ref in enumerate(texts):
        text = ref[...]
        t = ahead * SCALE + BIAS
        if k + 1 < len(texts):
            ahead = tile_dot(packed, texts[k + 1][...])
        count = text.shape[0] // ROWS
        mask = jnp.concatenate(lines[:count], axis=1)
        lines = lines[count:]
        sign = jnp.ones(t.shape, jnp.float32)
        if k == 0:
            own = jnp.concatenate([1.0 - 2.0 * picks[0], sign[:CAP, ROWS:]], axis=1)
            sign = jnp.concatenate([own, sign[CAP:]], axis=0)
            t = sign * t
        e = jnp.exp(-jnp.abs(t))
        s = jnp.where(t >= 0, 1.0, e) / (1.0 + e)
        slope = (s * (sign * mask) if k == 0 else s * mask).astype(jnp.bfloat16)
        total = total + jnp.dot(slope, text, preferred_element_type=jnp.float32)
    total = total.astype(jnp.bfloat16)
    width = total.shape[1]
    for k, o in enumerate(ZOFF):
        rows = pl.ds(pl.multiple_of(image_row(z, o) * CAP, CAP), CAP)
        load_ref[rows, :width] = total[k * CAP : (k + 1) * CAP, :]

    near, far = texts[:3], texts[3:]
    tasks = [(images[k : k + 2], far, False) for k in range(0, NZ, 2)]
    *totals, late = losses_of(tasks + [(images[NZ - 1 :], near, False)])
    for first, total in zip(range(0, NZ, 2), totals):
        for k in range(2):
            loss = total[:, k * ROWS : (k + 1) * ROWS]
            loss = loss + (late if first + k == NZ - 1 else early_ref[first + k : first + k + 1, :])
            parts = []
            for _ in range(3):
                part = loss.astype(jnp.bfloat16).astype(jnp.float32)
                loss = loss - part
                parts.append(part)
            parts.append(jnp.zeros((CAP - 3, ROWS), jnp.float32))
            beside = jnp.concatenate(parts, axis=0).astype(jnp.bfloat16)
            row = image_row(z, ZOFF[first + k])
            load_ref[pl.ds(pl.multiple_of(row * CAP, CAP), CAP), width:] = beside


def finish_kernel(load_ref, unit_ref, n_ref, keep_ref, msg_ref):
    width = unit_ref.shape[1]
    cut = width // 2
    total = load_ref[:CAP, :].astype(jnp.float32)
    for z in range(1, NZ):
        total = total + load_ref[z * CAP : (z + 1) * CAP, :].astype(jnp.float32)
    g = SCALE * total[:, :width]
    unit = unit_ref[...]
    grad = (g - unit * jnp.sum(unit * g, axis=1, keepdims=True)) / n_ref[:, :1]
    loss = total[0:1, width:] + total[1:2, width:] + total[2:3, width:]
    line = jnp.concatenate([loss, jnp.zeros((1, cut - ROWS), jnp.float32)], axis=1)
    keep_ref[:CAP, :] = grad[:, cut:]
    keep_ref[CAP:, :] = jnp.broadcast_to(line, (8, cut))
    msg_ref[:CAP, :] = grad[:, :cut]
    msg_ref[CAP:, :] = jnp.broadcast_to(line, (8, cut))


def spread_kernel(pos_ref, keep_ref, recv_ref, place_ref, learn_ref, out_ref):
    learner = pos_ref[5] == 1
    half = jnp.where(learner, keep_ref[:CAP, :], recv_ref[:CAP, :])
    pick = own_pick(place_ref[pl.ds(pos_ref[1] * (NX * NY) + pos_ref[4], 1), :])
    out_ref[...] = lax.dot_general(
        half, pick, (((0,), (0,)), ((), ())), precision=EXACT, preferred_element_type=jnp.float32
    )
    own, other = keep_ref[CAP : CAP + 1, :ROWS], recv_ref[CAP : CAP + 1, :ROWS]
    learn_ref[...] = jnp.where(learner, own - other, other - own)


def shards(image_features, text_features, norm_gain, up_weight, down_weight, text_head, sub_index):
    g_idx = lax.axis_index("grp")
    z_idx = lax.axis_index("z")
    x_idx = lax.axis_index("x")
    m_idx = lax.axis_index("yhi")
    l_idx = lax.axis_index("ylo")
    width = image_features.shape[1]
    rows = image_features.shape[0] // 2
    blocks = NZ * NX * NY
    cut = width // 2
    bf16 = jnp.bfloat16
    pos = [m_idx, z_idx, x_idx, m_idx * 2 + l_idx, (x_idx * 2 + l_idx) * 2 + m_idx, g_idx]
    pos = jnp.stack([p.astype(jnp.int32) for p in pos])
    cells = rows * width

    own_text, other_text, normed, own_x = front(
        pos, image_features, norm_gain, text_features, text_head[0]
    )
    recv_text = over_mp(other_text)
    own_img, other_img = image_mlp(pos, normed, own_x, up_weight[0].T, down_weight[0])
    other_img, recv_text = lax.optimization_barrier((other_img, recv_text))
    recv_img = over_mp(other_img)
    chosen, place_of = call(
        index_kernel, [], [sub_index.reshape(1, -1)], [shape((blocks, rows))] * 2, 100 << 20
    )
    own_img, place_of, chosen = lax.optimization_barrier((own_img, place_of, chosen))
    z_img, unit, n_img = call(
        image_unit_kernel,
        [],
        [own_img, recv_img],
        [shape((rows, width), bf16), shape((rows, width)), shape((rows, rows))],
        20 * cells,
    )
    (z_txt,) = call(
        text_unit_kernel, [], [own_text, recv_text], [shape((rows, width), bf16)], 20 * cells
    )
    line = [z_txt] + [over_plane(z_txt, shift, 0) for shift in (1, -1, 2)]
    z_img, line[1], line[2] = lax.optimization_barrier((z_img, line[1], line[2]))
    back, ahead = [z_img], [z_img]

    def z_step():
        back.append(over_z(back[-1], (1, 1)))
        ahead.append(over_z(ahead[-1], (-1, -1)))

    z_step()
    line[0], back[1], ahead[1] = lax.optimization_barrier((line[0], back[1], ahead[1]))
    (joined,) = call(join_kernel, [], line, [shape((4 * rows, width), bf16)], cells)
    text_back, text_ahead = over_plane(joined, 1, 1), over_plane(joined, -1, 1)
    z_step()
    z_step()
    last = over_z(jnp.where(g_idx == 0, back[3], ahead[3]), (1, -1))
    far_top = over_plane(text_back[: 2 * rows], 1, 1)
    far_low = over_plane(text_ahead[2 * rows :], -1, 1)
    texts = [joined, text_back, text_ahead, far_top, far_low]
    images = [z_img, back[1], ahead[1], back[2], ahead[2], back[3], ahead[3], last]

    all_img, n_text = NZ * rows, NX * NY * rows
    (early,) = call(
        early_kernel,
        [],
        images[:-1] + texts[:3],
        [shape((NZ, rows))],
        all_img * width * n_text,
        transcendentals=all_img * n_text // 2,
    )
    (load,) = call(
        pair_kernel,
        [pos],
        [chosen, place_of, early] + images + texts,
        [shape((NZ * CAP, width + rows), bf16)],
        (all_img + 4 * NZ * CAP) * width * n_text,
        transcendentals=all_img * n_text // 2,
    )
    load = lax.all_to_all(load, "z", 0, 0, tiled=True)
    unit_sub, n_sub = call(
        sub_unit_kernel,
        [pos],
        [unit, n_img, place_of],
        [shape((CAP, width)), shape((CAP, rows))],
        400 * cells,
    )
    keep, msg = call(
        finish_kernel, [], [load, unit_sub, n_sub], [shape((CAP + 8, cut))] * 2, 10 * cells
    )
    learn, image_grad = call(
        spread_kernel,
        [pos],
        [keep, swap_cores(msg), place_of],
        [shape((1, rows)), shape((cut, rows))],
        200 * cells,
    )
    return (learn.reshape(rows), image_grad.T)


def solution(mesh):
    fine = Mesh(mesh.devices.reshape(2, NZ, NX, 2, 2), AXES)
    dp = ("z", "x", "ylo")
    in_specs = (
        P(dp, None),
        P(dp, None),
        P("grp", None),
        P("grp", None, "yhi"),
        P("grp", "yhi", None),
        P("grp", "yhi", None),
        P(),
    )
    out_specs = (P(dp + ("yhi",)), P(dp + ("yhi",), "grp"))
    return jax.shard_map(shards, mesh=fine, in_specs=in_specs, out_specs=out_specs, check_vma=False)
```

```python
import jax
import jax.numpy as jnp
from jax import lax
from jax.experimental import pallas as pl
from jax.experimental.pallas import tpu as pltpu
from jax.sharding import Mesh, PartitionSpec as P

SCALE = 117.0
BIAS = -12.9
EPS = 1e-06
LOG2E = 1.4426950408889634
LN2 = 0.6931471805599453
NZ, NX, NY = 8, 4, 4
ROWS = 128
CAP = 32
AXES = ("grp", "z", "x", "ylo", "yhi")
ZOFF = (0, -1, 1, -2, 2, -3, 3, 4)
POFF = (0, -1, 1, 2)
EXACT = lax.Precision.HIGHEST


def place(g, z, x, y):
    return ((g * NZ + z) * NX + x) * NY + (y % 2) * 2 + y // 2


def permute(v, target, cores=(0, 1)):
    perm = [
        (place(g, z, x, y), place(*target(g, z, x, y)))
        for g in cores
        for z in range(NZ)
        for x in range(NX)
        for y in range(NY)
    ]
    return lax.ppermute(v, AXES, perm)


def over_mp(v):
    return permute(v, lambda g, z, x, y: (g, z, x, (y + 2) % NY))


def over_z(v, shifts, cores=(0, 1)):
    return permute(v, lambda g, z, x, y: (g, (z + shifts[g]) % NZ, x, y), cores)


def over_plane(v, shift, first):
    def target(g, z, x, y):
        if g == first:
            return (g, z, (x + shift) % NX, y)
        return (g, z, x, (y + shift) % NY)

    return permute(v, target)


def swap_cores(v):
    return permute(v, lambda g, z, x, y: (1 - g, z, x, y))


def shape(dims, dtype=jnp.float32):
    return jax.ShapeDtypeStruct(dims, dtype)


def call(kernel, scalars, arrays, outs, flops, mib=8, transcendentals=0, scratch=()):
    vmem = pl.BlockSpec(memory_space=pltpu.VMEM)
    return pl.pallas_call(
        kernel,
        in_specs=[pl.BlockSpec(memory_space=pltpu.SMEM)] * len(scalars) + [vmem] * len(arrays),
        out_specs=[vmem] * len(outs),
        out_shape=outs,
        scratch_shapes=scratch,
        compiler_params=pltpu.CompilerParams(vmem_limit_bytes=mib * 1024 * 1024),
        cost_estimate=pl.CostEstimate(
            flops=flops, bytes_accessed=1 << 20, transcendentals=transcendentals
        ),
    )(*scalars, *arrays)


def index_kernel(sub_ref, chosen_ref, place_ref):
    sub = sub_ref[...]
    line = lax.broadcasted_iota(jnp.int32, (ROWS, sub.shape[1]), 0)
    in_block = jnp.where((sub >> 7) == line, 1.0, 0.0).astype(jnp.bfloat16)
    at_off = jnp.where((sub & 127) == line, 1.0, 0.0).astype(jnp.bfloat16)
    chosen = lax.dot_general(
        in_block, at_off, (((1,), (1,)), ((), ())), preferred_element_type=jnp.float32
    )
    row = lax.broadcasted_iota(jnp.int32, (ROWS, ROWS), 0)
    col = lax.broadcasted_iota(jnp.int32, (ROWS, ROWS), 1)
    upper = jnp.where(row < col, 1.0, 0.0).astype(jnp.bfloat16)
    rank = jnp.dot(chosen.astype(jnp.bfloat16), upper, preferred_element_type=jnp.float32)
    chosen_ref[...] = chosen
    place_ref[...] = jnp.where(chosen > 0.5, rank, -1.0)


def split_rows(acc_ref, m, own_ref, other_ref):
    rows = own_ref.shape[0]
    own_ref[...] = acc_ref[pl.ds(pl.multiple_of(m * rows, rows), rows), :]
    other = acc_ref[pl.ds(pl.multiple_of((1 - m) * rows, rows), rows), :]
    other_ref[...] = other.astype(jnp.bfloat16)


CHUNK = 384


def chunk_copies(source, target, sems, first):
    return [
        pltpu.make_async_copy(
            source.at[:, pl.ds(start, CHUNK)], target.at[:, pl.ds(start, CHUNK)], sems.at[first + k]
        )
        for k, start in enumerate(range(0, target.shape[1], CHUNK))
    ]


def front_kernel(
    pos_ref, x_hbm, gain_hbm, text_hbm, head_hbm,
    own_ref, other_ref, normed_ref, own_x_ref,
    x_ref, gain_ref, text_ref, head_ref, acc_ref, sems,
):
    copies = [
        pltpu.make_async_copy(source, target, sems.at[k])
        for k, (source, target) in enumerate(
            [(x_hbm, x_ref), (gain_hbm, gain_ref), (text_hbm, text_ref)]
        )
    ]
    copies += chunk_copies(head_hbm, head_ref, sems, 3)
    for c in copies:
        c.start()
    m = pos_ref[0]
    rows = own_ref.shape[0]
    copies[0].wait()
    copies[1].wait()
    x = x_ref[...].astype(jnp.float32)
    mean = jnp.mean(x, axis=1, keepdims=True)
    gap = x - mean
    var = jnp.mean(gap * gap, axis=1, keepdims=True)
    normed_ref[...] = (gap * lax.rsqrt(var + EPS) * gain_ref[...]).astype(jnp.bfloat16)
    own_x_ref[...] = x_ref[pl.ds(pl.multiple_of(m * rows, rows), rows), :]
    copies[2].wait()
    depth = head_ref.shape[0]
    text = text_ref[...]
    part = jnp.where(m == 0, text[:, :depth], text[:, depth:])
    for k, start in enumerate(range(0, acc_ref.shape[1], CHUNK)):
        copies[3 + k].wait()
        acc_ref[:, start : start + CHUNK] = jnp.dot(
            part, head_ref[:, start : start + CHUNK], preferred_element_type=jnp.float32
        )
    split_rows(acc_ref, m, own_ref, other_ref)


def front(pos, x, gain, text, head):
    arrays = [x, gain, text, head]
    rows, width = x.shape
    half, bf16 = rows // 2, jnp.bfloat16
    vmem, hbm = pl.BlockSpec(memory_space=pltpu.VMEM), pl.BlockSpec(memory_space=pl.ANY)
    return pl.pallas_call(
        front_kernel,
        in_specs=[pl.BlockSpec(memory_space=pltpu.SMEM)] + [hbm] * len(arrays),
        out_specs=[vmem] * 4,
        out_shape=[
            shape((half, width)),
            shape((half, width), bf16),
            shape((rows, width), bf16),
            shape((half, width), bf16),
        ],
        scratch_shapes=[pltpu.VMEM(a.shape, a.dtype) for a in arrays]
        + [pltpu.VMEM((rows, width), jnp.float32), pltpu.SemaphoreType.DMA((3 + width // CHUNK,))],
        compiler_params=pltpu.CompilerParams(vmem_limit_bytes=52 * 1024 * 1024),
        cost_estimate=pl.CostEstimate(
            flops=2 * rows * width * head.shape[0], bytes_accessed=4 << 20, transcendentals=0
        ),
    )(pos, *arrays)


def mlp_kernel(
    pos_ref, normed_ref, own_x_ref, up_hbm, down_hbm, own_ref, other_ref,
    up_ref, down_ref, hidden_ref, acc_ref, sems,
):
    ups = chunk_copies(up_hbm, up_ref, sems, 0)
    downs = chunk_copies(down_hbm, down_ref, sems, len(ups))
    for c in ups + downs:
        c.start()
    for c in ups:
        c.wait()
    total, block = up_ref.shape[0], 512
    for start in range(0, total, block):
        stop = min(start + block, total)
        acc = lax.dot_general(
            normed_ref[...],
            up_ref[start:stop, :],
            (((1,), (1,)), ((), ())),
            preferred_element_type=jnp.float32,
        )
        hidden_ref[:, start:stop] = jax.nn.gelu(acc, approximate=True).astype(jnp.bfloat16)
    for k, start in enumerate(range(0, acc_ref.shape[1], CHUNK)):
        downs[k].wait()
        acc_ref[:, start : start + CHUNK] = jnp.dot(
            hidden_ref[...], down_ref[:, start : start + CHUNK], preferred_element_type=jnp.float32
        )
    split_rows(acc_ref, pos_ref[0], own_ref, other_ref)
    own_ref[...] = own_ref[...] + own_x_ref[...].astype(jnp.float32)


def image_mlp(pos, normed, own_x, up, down):
    rows, width = normed.shape
    half, hidden, bf16 = rows // 2, up.shape[0], jnp.bfloat16
    vmem, hbm = pl.BlockSpec(memory_space=pltpu.VMEM), pl.BlockSpec(memory_space=pl.ANY)
    return pl.pallas_call(
        mlp_kernel,
        in_specs=[pl.BlockSpec(memory_space=pltpu.SMEM), vmem, vmem, hbm, hbm],
        out_specs=[vmem, vmem],
        out_shape=[shape((half, width)), shape((half, width), bf16)],
        scratch_shapes=[
            pltpu.VMEM(up.shape, bf16),
            pltpu.VMEM(down.shape, bf16),
            pltpu.VMEM((rows, hidden), bf16),
            pltpu.VMEM((rows, width), jnp.float32),
            pltpu.SemaphoreType.DMA((2 * (width // CHUNK),)),
        ],
        compiler_params=pltpu.CompilerParams(vmem_limit_bytes=52 * 1024 * 1024),
        cost_estimate=pl.CostEstimate(
            flops=4 * rows * width * hidden, bytes_accessed=11 << 20, transcendentals=rows * hidden
        ),
    )(pos, normed, own_x, up, down)


def text_unit_kernel(own_ref, recv_ref, z_ref):
    e = own_ref[...] + recv_ref[...].astype(jnp.float32)
    n = jnp.sqrt(jnp.sum(e * e, axis=1, keepdims=True) + EPS)
    z_ref[...] = (e / n).astype(jnp.bfloat16)


def own_pick(place_row):
    slot = lax.broadcasted_iota(jnp.int32, (CAP, ROWS), 0).astype(jnp.float32)
    return jnp.where(place_row == slot, 1.0, 0.0)


def image_unit_kernel(own_ref, recv_ref, z_ref, unit_ref, n_ref):
    e = own_ref[...] + recv_ref[...].astype(jnp.float32)
    n = jnp.sqrt(jnp.sum(e * e, axis=1, keepdims=True) + EPS)
    unit = e / n
    z_ref[...] = unit.astype(jnp.bfloat16)
    unit_ref[...] = unit
    n_ref[...] = jnp.broadcast_to(n, n_ref.shape)


def sub_unit_kernel(pos_ref, unit_ref, n_ref, place_ref, unit_sub_ref, n_sub_ref):
    pick = own_pick(place_ref[pl.ds(pos_ref[1] * (NX * NY) + pos_ref[4], 1), :])
    unit_sub_ref[...] = jnp.dot(
        pick, unit_ref[...], precision=EXACT, preferred_element_type=jnp.float32
    )
    n_sub = jnp.dot(pick, n_ref[...], precision=EXACT, preferred_element_type=jnp.float32)
    n_sub_ref[...] = jnp.where(n_sub > 0.0, n_sub, 1.0)


def join_kernel(*refs):
    refs[-1][...] = jnp.concatenate([r[...] for r in refs[:-1]], axis=0)


def fold_terms(e):
    n = e.shape[0]
    while n > 1:
        n //= 2
        a, b = e[:n], e[n:]
        e = a + (b + a * b)
    return e[0]


def tile_dot(text, img):
    return lax.dot_general(text, img, (((1,), (1,)), ((), ())), preferred_element_type=jnp.float32)


def tile_loss(d, own):
    rows, width = d.shape
    d = d + BIAS / SCALE
    if own:
        row = lax.broadcasted_iota(jnp.int32, (ROWS, width), 0)
        col = lax.broadcasted_iota(jnp.int32, (ROWS, width), 1)
        d = jnp.concatenate([jnp.where(col == row, -d[:ROWS], d[:ROWS]), d[ROWS:]], axis=0)
    d = d.reshape(rows // 8, 8, width)
    high = jnp.sum(jnp.maximum(d, 0.0), axis=0)
    low = jnp.log1p(fold_terms(jnp.exp2(jnp.abs(d) * (-SCALE * LOG2E))))
    return high * SCALE + low


def losses_of(tasks):
    totals = [jnp.zeros((8, sum(r.shape[0] for r in g)), jnp.float32) for g, _, _ in tasks]
    waiting = None
    for number, (group, texts, own) in enumerate(tasks):
        img = [r[...] for r in group]
        img = img[0] if len(img) == 1 else jnp.concatenate(img, axis=0)
        for k, ref in enumerate(texts):
            d = tile_dot(ref[...], img)
            if waiting is not None:
                before, tile, diagonal = waiting
                totals[before] = totals[before] + tile_loss(tile, diagonal)
            waiting = (number, d, own and k == 0)
    before, tile, diagonal = waiting
    totals[before] = totals[before] + tile_loss(tile, diagonal)
    return [jnp.sum(t, axis=0, keepdims=True) for t in totals]


def image_row(z, offset):
    return lax.rem(z + (offset + NZ), NZ)


def early_kernel(*refs):
    images, texts, out_ref = refs[: NZ - 1], refs[NZ - 1 : -1], refs[-1]
    tasks = [(images[k : k + 2], texts, k == 0) for k in range(0, NZ - 1, 2)]
    for number, total in enumerate(losses_of(tasks)):
        for k in range(total.shape[1] // ROWS):
            row = 2 * number + k
            out_ref[row : row + 1, :] = total[:, k * ROWS : (k + 1) * ROWS]
    out_ref[NZ - 1 :, :] = jnp.zeros((1, ROWS), jnp.float32)


def pair_kernel(pos_ref, chosen_ref, place_ref, early_ref, *refs):
    images, texts, load_ref = refs[:NZ], refs[NZ:-1], refs[-1]
    z, x, y, xy = pos_ref[1], pos_ref[2], pos_ref[3], pos_ref[4]
    planes = NX * NY

    picks = [own_pick(place_ref[pl.ds(image_row(z, o) * planes + xy, 1), :]) for o in ZOFF]
    packed = jnp.concatenate(
        [
            jnp.dot(p.astype(jnp.bfloat16), images[k][...], preferred_element_type=jnp.float32)
            for k, p in enumerate(picks)
        ],
        axis=0,
    ).astype(jnp.bfloat16)

    def text_row(dx, dy):
        tx, ty = lax.rem(x + (dx + NX), NX), lax.rem(y + (dy + NY), NY)
        row = z * planes + tx * NY + lax.rem(ty, 2) * 2 + ty // 2
        return chosen_ref[pl.ds(row, 1), :]

    lines = [text_row(dx, dy) for dx in POFF for dy in POFF]
    total = jnp.zeros(packed.shape, jnp.float32)
    ahead = tile_dot(packed, texts[0][...])
    for k, ref in enumerate(texts):
        text = ref[...]
        t = ahead * SCALE + BIAS
        if k + 1 < len(texts):
            ahead = tile_dot(packed, texts[k + 1][...])
        count = text.shape[0] // ROWS
        mask = jnp.concatenate(lines[:count], axis=1)
        lines = lines[count:]
        sign = jnp.ones(t.shape, jnp.float32)
        if k == 0:
            own = jnp.concatenate([1.0 - 2.0 * picks[0], sign[:CAP, ROWS:]], axis=1)
            sign = jnp.concatenate([own, sign[CAP:]], axis=0)
            t = sign * t
        e = jnp.exp(-jnp.abs(t))
        s = jnp.where(t >= 0, 1.0, e) / (1.0 + e)
        slope = (s * (sign * mask) if k == 0 else s * mask).astype(jnp.bfloat16)
        total = total + jnp.dot(slope, text, preferred_element_type=jnp.float32)
    total = total.astype(jnp.bfloat16)
    width = total.shape[1]
    for k, o in enumerate(ZOFF):
        rows = pl.ds(pl.multiple_of(image_row(z, o) * CAP, CAP), CAP)
        load_ref[rows, :width] = total[k * CAP : (k + 1) * CAP, :]

    near, far = texts[:3], texts[3:]
    tasks = [(images[k : k + 2], far, False) for k in range(0, NZ, 2)]
    *totals, late = losses_of(tasks + [(images[NZ - 1 :], near, False)])
    for first, total in zip(range(0, NZ, 2), totals):
        for k in range(2):
            loss = total[:, k * ROWS : (k + 1) * ROWS]
            loss = loss + (late if first + k == NZ - 1 else early_ref[first + k : first + k + 1, :])
            parts = []
            for _ in range(3):
                part = loss.astype(jnp.bfloat16).astype(jnp.float32)
                loss = loss - part
                parts.append(part)
            parts.append(jnp.zeros((CAP - 3, ROWS), jnp.float32))
            beside = jnp.concatenate(parts, axis=0).astype(jnp.bfloat16)
            row = image_row(z, ZOFF[first + k])
            load_ref[pl.ds(pl.multiple_of(row * CAP, CAP), CAP), width:] = beside


def finish_kernel(load_ref, unit_ref, n_ref, keep_ref, msg_ref):
    width = unit_ref.shape[1]
    cut = width // 2
    total = load_ref[:CAP, :].astype(jnp.float32)
    for z in range(1, NZ):
        total = total + load_ref[z * CAP : (z + 1) * CAP, :].astype(jnp.float32)
    g = SCALE * total[:, :width]
    unit = unit_ref[...]
    grad = (g - unit * jnp.sum(unit * g, axis=1, keepdims=True)) / n_ref[:, :1]
    loss = total[0:1, width:] + total[1:2, width:] + total[2:3, width:]
    line = jnp.concatenate([loss, jnp.zeros((1, cut - ROWS), jnp.float32)], axis=1)
    keep_ref[:CAP, :] = grad[:, cut:]
    keep_ref[CAP:, :] = jnp.broadcast_to(line, (8, cut))
    msg_ref[:CAP, :] = grad[:, :cut]
    msg_ref[CAP:, :] = jnp.broadcast_to(line, (8, cut))


def spread_kernel(pos_ref, keep_ref, recv_ref, place_ref, learn_ref, out_ref):
    learner = pos_ref[5] == 1
    half = jnp.where(learner, keep_ref[:CAP, :], recv_ref[:CAP, :])
    pick = own_pick(place_ref[pl.ds(pos_ref[1] * (NX * NY) + pos_ref[4], 1), :])
    out_ref[...] = lax.dot_general(
        half, pick, (((0,), (0,)), ((), ())), precision=EXACT, preferred_element_type=jnp.float32
    )
    own, other = keep_ref[CAP : CAP + 1, :ROWS], recv_ref[CAP : CAP + 1, :ROWS]
    learn_ref[...] = jnp.where(learner, own - other, other - own)


def shards(image_features, text_features, norm_gain, up_weight, down_weight, text_head, sub_index):
    g_idx = lax.axis_index("grp")
    z_idx = lax.axis_index("z")
    x_idx = lax.axis_index("x")
    m_idx = lax.axis_index("yhi")
    l_idx = lax.axis_index("ylo")
    width = image_features.shape[1]
    rows = image_features.shape[0] // 2
    blocks = NZ * NX * NY
    cut = width // 2
    bf16 = jnp.bfloat16
    pos = [m_idx, z_idx, x_idx, m_idx * 2 + l_idx, (x_idx * 2 + l_idx) * 2 + m_idx, g_idx]
    pos = jnp.stack([p.astype(jnp.int32) for p in pos])
    cells = rows * width

    own_text, other_text, normed, own_x = front(
        pos, image_features, norm_gain, text_features, text_head[0]
    )
    recv_text = over_mp(other_text)
    own_img, other_img = image_mlp(pos, normed, own_x, up_weight[0].T, down_weight[0])
    other_img, recv_text = lax.optimization_barrier((other_img, recv_text))
    recv_img = over_mp(other_img)
    chosen, place_of = call(
        index_kernel, [], [sub_index.reshape(1, -1)], [shape((blocks, rows))] * 2, 100 << 20
    )
    own_img, place_of, chosen = lax.optimization_barrier((own_img, place_of, chosen))
    z_img, unit, n_img = call(
        image_unit_kernel,
        [],
        [own_img, recv_img],
        [shape((rows, width), bf16), shape((rows, width)), shape((rows, rows))],
        20 * cells,
    )
    (z_txt,) = call(
        text_unit_kernel, [], [own_text, recv_text], [shape((rows, width), bf16)], 20 * cells
    )
    line = [z_txt] + [over_plane(z_txt, shift, 0) for shift in (1, -1, 2)]
    z_img, line[1], line[2] = lax.optimization_barrier((z_img, line[1], line[2]))
    back, ahead = [z_img], [z_img]

    def z_step():
        back.append(over_z(back[-1], (1, 1)))
        ahead.append(over_z(ahead[-1], (-1, -1)))

    z_step()
    line[0], back[1], ahead[1] = lax.optimization_barrier((line[0], back[1], ahead[1]))
    (joined,) = call(join_kernel, [], line, [shape((4 * rows, width), bf16)], cells)
    text_back, text_ahead = over_plane(joined, 1, 1), over_plane(joined, -1, 1)
    z_step()
    z_step()
    last = over_z(jnp.where(g_idx == 0, back[3], ahead[3]), (1, -1))
    far_top = over_plane(text_back[: 2 * rows], 1, 1)
    far_low = over_plane(text_ahead[2 * rows :], -1, 1)
    texts = [joined, text_back, text_ahead, far_top, far_low]
    images = [z_img, back[1], ahead[1], back[2], ahead[2], back[3], ahead[3], last]

    all_img, n_text = NZ * rows, NX * NY * rows
    (early,) = call(
        early_kernel,
        [],
        images[:-1] + texts[:3],
        [shape((NZ, rows))],
        all_img * width * n_text,
        transcendentals=all_img * n_text // 2,
    )
    (load,) = call(
        pair_kernel,
        [pos],
        [chosen, place_of, early] + images + texts,
        [shape((NZ * CAP, width + rows), bf16)],
        (all_img + 4 * NZ * CAP) * width * n_text,
        transcendentals=all_img * n_text // 2,
    )
    load = lax.all_to_all(load, "z", 0, 0, tiled=True)
    unit_sub, n_sub = call(
        sub_unit_kernel,
        [pos],
        [unit, n_img, place_of],
        [shape((CAP, width)), shape((CAP, rows))],
        400 * cells,
    )
    keep, msg = call(
        finish_kernel, [], [load, unit_sub, n_sub], [shape((CAP + 8, cut))] * 2, 10 * cells
    )
    learn, image_grad = call(
        spread_kernel,
        [pos],
        [keep, swap_cores(msg), place_of],
        [shape((1, rows)), shape((cut, rows))],
        200 * cells,
    )
    return (learn.reshape(rows), image_grad.T)


def solution(mesh):
    fine = Mesh(mesh.devices.reshape(2, NZ, NX, 2, 2), AXES)
    dp = ("z", "x", "ylo")
    in_specs = (
        P(dp, None),
        P(dp, None),
        P("grp", None),
        P("grp", None, "yhi"),
        P("grp", "yhi", None),
        P("grp", "yhi", None),
        P(),
    )
    out_specs = (P(dp + ("yhi",)), P(dp + ("yhi",), "grp"))
    return jax.shard_map(shards, mesh=fine, in_specs=in_specs, out_specs=out_specs, check_vma=False)
```

```python
import jax
import jax.numpy as jnp
from jax import lax
from jax.experimental import pallas as pl
from jax.experimental.pallas import tpu as pltpu
from jax.sharding import Mesh, PartitionSpec as P

SCALE = 117.0
BIAS = -12.9
EPS = 1e-06
LOG2E = 1.4426950408889634
LN2 = 0.6931471805599453
NZ, NX, NY = 8, 4, 4
ROWS = 128
CAP = 32
AXES = ("grp", "z", "x", "ylo", "yhi")
ZOFF = (0, -1, 1, -2, 2, -3, 3, 4)
POFF = (0, -1, 1, 2)
EXACT = lax.Precision.HIGHEST


def place(g, z, x, y):
    return ((g * NZ + z) * NX + x) * NY + (y % 2) * 2 + y // 2


def permute(v, target, cores=(0, 1)):
    perm = [
        (place(g, z, x, y), place(*target(g, z, x, y)))
        for g in cores
        for z in range(NZ)
        for x in range(NX)
        for y in range(NY)
    ]
    return lax.ppermute(v, AXES, perm)


def over_mp(v):
    return permute(v, lambda g, z, x, y: (g, z, x, (y + 2) % NY))


def over_z(v, shifts, cores=(0, 1)):
    return permute(v, lambda g, z, x, y: (g, (z + shifts[g]) % NZ, x, y), cores)


def over_plane(v, shift, first):
    def target(g, z, x, y):
        if g == first:
            return (g, z, (x + shift) % NX, y)
        return (g, z, x, (y + shift) % NY)

    return permute(v, target)


def swap_cores(v):
    return permute(v, lambda g, z, x, y: (1 - g, z, x, y))


def shape(dims, dtype=jnp.float32):
    return jax.ShapeDtypeStruct(dims, dtype)


def call(kernel, scalars, arrays, outs, flops, mib=8, transcendentals=0, scratch=()):
    vmem = pl.BlockSpec(memory_space=pltpu.VMEM)
    return pl.pallas_call(
        kernel,
        in_specs=[pl.BlockSpec(memory_space=pltpu.SMEM)] * len(scalars) + [vmem] * len(arrays),
        out_specs=[vmem] * len(outs),
        out_shape=outs,
        scratch_shapes=scratch,
        compiler_params=pltpu.CompilerParams(vmem_limit_bytes=mib * 1024 * 1024),
        cost_estimate=pl.CostEstimate(
            flops=flops, bytes_accessed=1 << 20, transcendentals=transcendentals
        ),
    )(*scalars, *arrays)


def index_kernel(sub_ref, chosen_ref, place_ref):
    sub = sub_ref[...]
    line = lax.broadcasted_iota(jnp.int32, (ROWS, sub.shape[1]), 0)
    in_block = jnp.where((sub >> 7) == line, 1.0, 0.0).astype(jnp.bfloat16)
    at_off = jnp.where((sub & 127) == line, 1.0, 0.0).astype(jnp.bfloat16)
    chosen = lax.dot_general(
        in_block, at_off, (((1,), (1,)), ((), ())), preferred_element_type=jnp.float32
    )
    row = lax.broadcasted_iota(jnp.int32, (ROWS, ROWS), 0)
    col = lax.broadcasted_iota(jnp.int32, (ROWS, ROWS), 1)
    upper = jnp.where(row < col, 1.0, 0.0).astype(jnp.bfloat16)
    rank = jnp.dot(chosen.astype(jnp.bfloat16), upper, preferred_element_type=jnp.float32)
    chosen_ref[...] = chosen
    place_ref[...] = jnp.where(chosen > 0.5, rank, -1.0)


def split_rows(acc_ref, m, own_ref, other_ref):
    rows = own_ref.shape[0]
    own_ref[...] = acc_ref[pl.ds(pl.multiple_of(m * rows, rows), rows), :]
    other = acc_ref[pl.ds(pl.multiple_of((1 - m) * rows, rows), rows), :]
    other_ref[...] = other.astype(jnp.bfloat16)


def text_kernel(
    pos_ref, text_hbm, head_hbm, own_ref, other_ref, text_ref, head_ref, acc_ref, sems
):
    copies = [
        pltpu.make_async_copy(text_hbm, text_ref, sems.at[0]),
        pltpu.make_async_copy(head_hbm, head_ref, sems.at[1]),
    ]
    for c in copies:
        c.start()
    for c in copies:
        c.wait()
    depth = head_ref.shape[0]
    m = pos_ref[0]
    text = text_ref[...]
    part = jnp.where(m == 0, text[:, :depth], text[:, depth:])
    acc_ref[...] = jnp.dot(part, head_ref[...], preferred_element_type=jnp.float32)
    split_rows(acc_ref, m, own_ref, other_ref)


def mlp_kernel(
    pos_ref, x_hbm, gain_hbm, up_hbm, down_hbm, own_ref, other_ref,
    x_ref, gain_ref, up_ref, down_ref, normed_ref, hidden_ref, acc_ref, sems,
):
    copies = [
        pltpu.make_async_copy(source, target, sems.at[k])
        for k, (source, target) in enumerate(
            [(x_hbm, x_ref), (gain_hbm, gain_ref), (up_hbm, up_ref), (down_hbm, down_ref)]
        )
    ]
    for c in copies[:3]:
        c.start()
    m = pos_ref[0]
    rows = own_ref.shape[0]
    copies[0].wait()
    copies[1].wait()
    x = x_ref[...].astype(jnp.float32)
    mean = jnp.mean(x, axis=1, keepdims=True)
    gap = x - mean
    var = jnp.mean(gap * gap, axis=1, keepdims=True)
    normed_ref[...] = (gap * lax.rsqrt(var + EPS) * gain_ref[...]).astype(jnp.bfloat16)
    copies[2].wait()
    copies[3].start()
    total, block = up_ref.shape[0], 512
    for start in range(0, total, block):
        stop = min(start + block, total)
        acc = lax.dot_general(
            normed_ref[...],
            up_ref[start:stop, :],
            (((1,), (1,)), ((), ())),
            preferred_element_type=jnp.float32,
        )
        hidden_ref[:, start:stop] = jax.nn.gelu(acc, approximate=True).astype(jnp.bfloat16)
    copies[3].wait()
    block = 384
    for start in range(0, acc_ref.shape[1], block):
        acc_ref[:, start : start + block] = jnp.dot(
            hidden_ref[...], down_ref[:, start : start + block], preferred_element_type=jnp.float32
        )
    split_rows(acc_ref, m, own_ref, other_ref)
    x = x_ref[pl.ds(pl.multiple_of(m * rows, rows), rows), :]
    own_ref[...] = own_ref[...] + x.astype(jnp.float32)


def from_hbm(kernel, pos, arrays, rows, width, scratch, flops):
    vmem, hbm = pl.BlockSpec(memory_space=pltpu.VMEM), pl.BlockSpec(memory_space=pl.ANY)
    return pl.pallas_call(
        kernel,
        in_specs=[pl.BlockSpec(memory_space=pltpu.SMEM)] + [hbm] * len(arrays),
        out_specs=[vmem, vmem],
        out_shape=[shape((rows, width)), shape((rows, width), jnp.bfloat16)],
        scratch_shapes=[pltpu.VMEM(a.shape, a.dtype) for a in arrays]
        + scratch
        + [pltpu.VMEM((2 * rows, width), jnp.float32), pltpu.SemaphoreType.DMA((len(arrays),))],
        compiler_params=pltpu.CompilerParams(vmem_limit_bytes=52 * 1024 * 1024),
        cost_estimate=pl.CostEstimate(flops=flops, bytes_accessed=11 << 20, transcendentals=0),
    )(pos, *arrays)


def text_unit_kernel(own_ref, recv_ref, z_ref):
    e = own_ref[...] + recv_ref[...].astype(jnp.float32)
    n = jnp.sqrt(jnp.sum(e * e, axis=1, keepdims=True) + EPS)
    z_ref[...] = (e / n).astype(jnp.bfloat16)


def own_pick(place_row):
    slot = lax.broadcasted_iota(jnp.int32, (CAP, ROWS), 0).astype(jnp.float32)
    return jnp.where(place_row == slot, 1.0, 0.0)


def image_unit_kernel(own_ref, recv_ref, z_ref, unit_ref, n_ref):
    e = own_ref[...] + recv_ref[...].astype(jnp.float32)
    n = jnp.sqrt(jnp.sum(e * e, axis=1, keepdims=True) + EPS)
    unit = e / n
    z_ref[...] = unit.astype(jnp.bfloat16)
    unit_ref[...] = unit
    n_ref[...] = jnp.broadcast_to(n, n_ref.shape)


def sub_unit_kernel(pos_ref, unit_ref, n_ref, place_ref, unit_sub_ref, n_sub_ref):
    pick = own_pick(place_ref[pl.ds(pos_ref[1] * (NX * NY) + pos_ref[4], 1), :])
    unit_sub_ref[...] = jnp.dot(
        pick, unit_ref[...], precision=EXACT, preferred_element_type=jnp.float32
    )
    n_sub = jnp.dot(pick, n_ref[...], precision=EXACT, preferred_element_type=jnp.float32)
    n_sub_ref[...] = jnp.where(n_sub > 0.0, n_sub, 1.0)


def join_kernel(*refs):
    refs[-1][...] = jnp.concatenate([r[...] for r in refs[:-1]], axis=0)


def fold_terms(e):
    n = e.shape[0]
    while n > 1:
        n //= 2
        a, b = e[:n], e[n:]
        e = a + (b + a * b)
    return e[0]


def tile_dot(text, img):
    return lax.dot_general(text, img, (((1,), (1,)), ((), ())), preferred_element_type=jnp.float32)


def tile_loss(d, own):
    rows, width = d.shape
    d = d + BIAS / SCALE
    if own:
        row = lax.broadcasted_iota(jnp.int32, (ROWS, width), 0)
        col = lax.broadcasted_iota(jnp.int32, (ROWS, width), 1)
        d = jnp.concatenate([jnp.where(col == row, -d[:ROWS], d[:ROWS]), d[ROWS:]], axis=0)
    d = d.reshape(rows // 8, 8, width)
    high = jnp.sum(jnp.maximum(d, 0.0), axis=0)
    low = jnp.log1p(fold_terms(jnp.exp2(jnp.abs(d) * (-SCALE * LOG2E))))
    return high * SCALE + low


def losses_of(tasks):
    totals = [jnp.zeros((8, sum(r.shape[0] for r in g)), jnp.float32) for g, _, _ in tasks]
    waiting = None
    for number, (group, texts, own) in enumerate(tasks):
        img = [r[...] for r in group]
        img = img[0] if len(img) == 1 else jnp.concatenate(img, axis=0)
        for k, ref in enumerate(texts):
            d = tile_dot(ref[...], img)
            if waiting is not None:
                before, tile, diagonal = waiting
                totals[before] = totals[before] + tile_loss(tile, diagonal)
            waiting = (number, d, own and k == 0)
    before, tile, diagonal = waiting
    totals[before] = totals[before] + tile_loss(tile, diagonal)
    return [jnp.sum(t, axis=0, keepdims=True) for t in totals]


def image_row(z, offset):
    return lax.rem(z + (offset + NZ), NZ)


def early_kernel(*refs):
    images, texts, out_ref = refs[: NZ - 1], refs[NZ - 1 : -1], refs[-1]
    tasks = [(images[k : k + 2], texts, k == 0) for k in range(0, NZ - 1, 2)]
    for number, total in enumerate(losses_of(tasks)):
        for k in range(total.shape[1] // ROWS):
            row = 2 * number + k
            out_ref[row : row + 1, :] = total[:, k * ROWS : (k + 1) * ROWS]
    out_ref[NZ - 1 :, :] = jnp.zeros((1, ROWS), jnp.float32)


def pair_kernel(pos_ref, chosen_ref, place_ref, early_ref, *refs):
    images, texts, load_ref = refs[:NZ], refs[NZ:-1], refs[-1]
    z, x, y, xy = pos_ref[1], pos_ref[2], pos_ref[3], pos_ref[4]
    planes = NX * NY

    picks = [own_pick(place_ref[pl.ds(image_row(z, o) * planes + xy, 1), :]) for o in ZOFF]
    packed = jnp.concatenate(
        [
            jnp.dot(p.astype(jnp.bfloat16), images[k][...], preferred_element_type=jnp.float32)
            for k, p in enumerate(picks)
        ],
        axis=0,
    ).astype(jnp.bfloat16)

    def text_row(dx, dy):
        tx, ty = lax.rem(x + (dx + NX), NX), lax.rem(y + (dy + NY), NY)
        row = z * planes + tx * NY + lax.rem(ty, 2) * 2 + ty // 2
        return chosen_ref[pl.ds(row, 1), :]

    lines = [text_row(dx, dy) for dx in POFF for dy in POFF]
    total = jnp.zeros(packed.shape, jnp.float32)
    ahead = tile_dot(packed, texts[0][...])
    for k, ref in enumerate(texts):
        text = ref[...]
        t = ahead * SCALE + BIAS
        if k + 1 < len(texts):
            ahead = tile_dot(packed, texts[k + 1][...])
        count = text.shape[0] // ROWS
        mask = jnp.concatenate(lines[:count], axis=1)
        lines = lines[count:]
        sign = jnp.ones(t.shape, jnp.float32)
        if k == 0:
            own = jnp.concatenate([1.0 - 2.0 * picks[0], sign[:CAP, ROWS:]], axis=1)
            sign = jnp.concatenate([own, sign[CAP:]], axis=0)
            t = sign * t
        e = jnp.exp(-jnp.abs(t))
        s = jnp.where(t >= 0, 1.0, e) / (1.0 + e)
        slope = (s * (sign * mask) if k == 0 else s * mask).astype(jnp.bfloat16)
        total = total + jnp.dot(slope, text, preferred_element_type=jnp.float32)
    total = total.astype(jnp.bfloat16)
    width = total.shape[1]
    for k, o in enumerate(ZOFF):
        rows = pl.ds(pl.multiple_of(image_row(z, o) * CAP, CAP), CAP)
        load_ref[rows, :width] = total[k * CAP : (k + 1) * CAP, :]

    near, far = texts[:3], texts[3:]
    tasks = [(images[k : k + 2], far, False) for k in range(0, NZ, 2)]
    *totals, late = losses_of(tasks + [(images[NZ - 1 :], near, False)])
    for first, total in zip(range(0, NZ, 2), totals):
        for k in range(2):
            loss = total[:, k * ROWS : (k + 1) * ROWS]
            loss = loss + (late if first + k == NZ - 1 else early_ref[first + k : first + k + 1, :])
            parts = []
            for _ in range(3):
                part = loss.astype(jnp.bfloat16).astype(jnp.float32)
                loss = loss - part
                parts.append(part)
            parts.append(jnp.zeros((CAP - 3, ROWS), jnp.float32))
            beside = jnp.concatenate(parts, axis=0).astype(jnp.bfloat16)
            row = image_row(z, ZOFF[first + k])
            load_ref[pl.ds(pl.multiple_of(row * CAP, CAP), CAP), width:] = beside


def finish_kernel(load_ref, unit_ref, n_ref, keep_ref, msg_ref):
    width = unit_ref.shape[1]
    cut = width // 2
    total = load_ref[:CAP, :].astype(jnp.float32)
    for z in range(1, NZ):
        total = total + load_ref[z * CAP : (z + 1) * CAP, :].astype(jnp.float32)
    g = SCALE * total[:, :width]
    unit = unit_ref[...]
    grad = (g - unit * jnp.sum(unit * g, axis=1, keepdims=True)) / n_ref[:, :1]
    loss = total[0:1, width:] + total[1:2, width:] + total[2:3, width:]
    line = jnp.concatenate([loss, jnp.zeros((1, cut - ROWS), jnp.float32)], axis=1)
    keep_ref[:CAP, :] = grad[:, cut:]
    keep_ref[CAP:, :] = jnp.broadcast_to(line, (8, cut))
    msg_ref[:CAP, :] = grad[:, :cut]
    msg_ref[CAP:, :] = jnp.broadcast_to(line, (8, cut))


def spread_kernel(pos_ref, keep_ref, recv_ref, place_ref, learn_ref, out_ref):
    learner = pos_ref[5] == 1
    half = jnp.where(learner, keep_ref[:CAP, :], recv_ref[:CAP, :])
    pick = own_pick(place_ref[pl.ds(pos_ref[1] * (NX * NY) + pos_ref[4], 1), :])
    out_ref[...] = lax.dot_general(
        half, pick, (((0,), (0,)), ((), ())), precision=EXACT, preferred_element_type=jnp.float32
    )
    own, other = keep_ref[CAP : CAP + 1, :ROWS], recv_ref[CAP : CAP + 1, :ROWS]
    learn_ref[...] = jnp.where(learner, own - other, other - own)


def shards(image_features, text_features, norm_gain, up_weight, down_weight, text_head, sub_index):
    g_idx = lax.axis_index("grp")
    z_idx = lax.axis_index("z")
    x_idx = lax.axis_index("x")
    m_idx = lax.axis_index("yhi")
    l_idx = lax.axis_index("ylo")
    width = image_features.shape[1]
    rows = image_features.shape[0] // 2
    blocks = NZ * NX * NY
    cut = width // 2
    bf16 = jnp.bfloat16
    pos = [m_idx, z_idx, x_idx, m_idx * 2 + l_idx, (x_idx * 2 + l_idx) * 2 + m_idx, g_idx]
    pos = jnp.stack([p.astype(jnp.int32) for p in pos])
    cells = rows * width

    own_text, other_text = from_hbm(
        text_kernel, pos, [text_features, text_head[0]], rows, width, [], 2 * cells * width
    )
    recv_text = over_mp(other_text)
    features, own_text = lax.optimization_barrier((image_features, own_text))
    hidden = up_weight.shape[2]
    own_img, other_img = from_hbm(
        mlp_kernel,
        pos,
        [features, norm_gain, up_weight[0].T, down_weight[0]],
        rows,
        width,
        [pltpu.VMEM((2 * rows, width), bf16), pltpu.VMEM((2 * rows, hidden), bf16)],
        8 * cells * hidden,
    )
    other_img, recv_text = lax.optimization_barrier((other_img, recv_text))
    recv_img = over_mp(other_img)
    chosen, place_of = call(
        index_kernel, [], [sub_index.reshape(1, -1)], [shape((blocks, rows))] * 2, 100 << 20
    )
    own_img, place_of, chosen = lax.optimization_barrier((own_img, place_of, chosen))
    z_img, unit, n_img = call(
        image_unit_kernel,
        [],
        [own_img, recv_img],
        [shape((rows, width), bf16), shape((rows, width)), shape((rows, rows))],
        20 * cells,
    )
    (z_txt,) = call(
        text_unit_kernel, [], [own_text, recv_text], [shape((rows, width), bf16)], 20 * cells
    )
    line = [z_txt] + [over_plane(z_txt, shift, 0) for shift in (1, -1, 2)]
    z_img, line[1], line[2] = lax.optimization_barrier((z_img, line[1], line[2]))
    back, ahead = [z_img], [z_img]

    def z_step():
        back.append(over_z(back[-1], (1, 1)))
        ahead.append(over_z(ahead[-1], (-1, -1)))

    z_step()
    line[0], back[1], ahead[1] = lax.optimization_barrier((line[0], back[1], ahead[1]))
    (joined,) = call(join_kernel, [], line, [shape((4 * rows, width), bf16)], cells)
    text_back, text_ahead = over_plane(joined, 1, 1), over_plane(joined, -1, 1)
    z_step()
    z_step()
    last = over_z(jnp.where(g_idx == 0, back[3], ahead[3]), (1, -1))
    far = over_plane(text_ahead, -1, 1)
    texts = [joined, text_back, text_ahead, far]
    images = [z_img, back[1], ahead[1], back[2], ahead[2], back[3], ahead[3], last]

    all_img, n_text = NZ * rows, NX * NY * rows
    (early,) = call(
        early_kernel,
        [],
        images[:-1] + texts[:3],
        [shape((NZ, rows))],
        all_img * width * n_text,
        transcendentals=all_img * n_text // 2,
    )
    (load,) = call(
        pair_kernel,
        [pos],
        [chosen, place_of, early] + images + texts,
        [shape((NZ * CAP, width + rows), bf16)],
        (all_img + 4 * NZ * CAP) * width * n_text,
        transcendentals=all_img * n_text // 2,
    )
    load = lax.all_to_all(load, "z", 0, 0, tiled=True)
    unit_sub, n_sub = call(
        sub_unit_kernel,
        [pos],
        [unit, n_img, place_of],
        [shape((CAP, width)), shape((CAP, rows))],
        400 * cells,
    )
    keep, msg = call(
        finish_kernel, [], [load, unit_sub, n_sub], [shape((CAP + 8, cut))] * 2, 10 * cells
    )
    learn, image_grad = call(
        spread_kernel,
        [pos],
        [keep, swap_cores(msg), place_of],
        [shape((1, rows)), shape((cut, rows))],
        200 * cells,
    )
    return (learn.reshape(rows), image_grad.T)


def solution(mesh):
    fine = Mesh(mesh.devices.reshape(2, NZ, NX, 2, 2), AXES)
    dp = ("z", "x", "ylo")
    in_specs = (
        P(dp, None),
        P(dp, None),
        P("grp", None),
        P("grp", None, "yhi"),
        P("grp", "yhi", None),
        P("grp", "yhi", None),
        P(),
    )
    out_specs = (P(dp + ("yhi",)), P(dp + ("yhi",), "grp"))
    return jax.shard_map(shards, mesh=fine, in_specs=in_specs, out_specs=out_specs, check_vma=False)
```
